256 devices in a mesh: dp: 8 (over x, core), proto: 32 (over y, z).
Axes of the slice: x: 4, y: 4, z: 8, core: 2. Of those that a mesh axis runs over, the one named last changes fastest.
Arguments:
- features: bfloat16 [16384, 256], P('dp'), may hold values from -60 to 60
- prototypes: bfloat16 [32768, 256], P('proto'), may hold values from -50 to 50
- sibling_view: int32 [16384], P('dp'), may hold values from 0 to 2047, as said below
- q_seed: int32 [256, 32], replicated, may hold values from -8 to 7
Outputs:
- feature_grad: float32 [16384, 256], P(('dp', 'proto'))
- proto_grad: float32 [32768, 256], P('proto')
The draws below stay inside these ranges and needn't reach their ends.
Inputs may be any that keep to these rules, and one draw needn't show every extreme that they name: Within each data group of 2048 rows the pairing is a perfect matching: sibling_view[sibling_view[b]] = b and sibling_view[b] != b.
All inputs are finite; a program needn't handle non-finite values.
Results may differ from the reference program's by a relative error of at most 0.0024.
Values sent between devices are 32-bit elements; how exact they have to be, the bound alone decides.
No kernel may reach another device: no remote copies, remote signals or barrier semaphores. Data moves between devices by JAX's collectives and lax.ppermute only.
A program may use at most 128 MiB of HBM per device.

```python
import math
import jax
import jax.numpy as jnp
from jax import lax

ROWS = 2048
FEAT = 256
RANK = 32
SINK = 3
PROTOS = 32768
TOTAL_ROWS = 16384


centre_count = 16


def shared_directions(key):
    centre_key = jax.random.fold_in(jax.random.fold_in(key, 101), 0)
    centres = jax.random.truncated_normal(centre_key, -4.0, 4.0, (centre_count, FEAT), jnp.float32)
    return centres


def draw_features(key, part):
    centres = shared_directions(key)
    key = jax.random.fold_in(key, 11)
    pick_key, strength_key, noise_key = jax.random.split(key, 3)
    groups = TOTAL_ROWS // ROWS
    pick = jax.random.randint(pick_key, (TOTAL_ROWS,), 0, centre_count).astype(jnp.int32)
    strength = jnp.exp(jax.random.uniform(strength_key, (groups, centre_count), jnp.float32, math.log(0.15), math.log(0.9)))
    owner = (jnp.arange(TOTAL_ROWS) // ROWS).astype(jnp.int32)
    row_strength = strength.reshape(-1)[owner * centre_count + pick]
    lean = row_strength[:, None] * centres[pick]
    noise = jax.random.truncated_normal(noise_key, -4.0, 4.0, (TOTAL_ROWS, FEAT), jnp.float32)
    value_rows = noise + lean
    return value_rows.astype(jnp.bfloat16)


def draw_prototypes(key, part):
    centres = shared_directions(key)
    key = jax.random.fold_in(key, 13)
    pick_key, lean_key, noise_key = jax.random.split(key, 3)
    pick = jax.random.randint(pick_key, (PROTOS,), 0, centre_count).astype(jnp.int32)
    amount = jax.random.uniform(lean_key, (PROTOS, 1), jnp.float32, 0.0, 0.6)
    lean = amount * centres[pick]
    noise = jax.random.truncated_normal(noise_key, -4.0, 4.0, (PROTOS, FEAT), jnp.float32)
    value_rows = noise + lean
    return value_rows.astype(jnp.bfloat16)


def draw_sibling_view(key, part):
    key = jax.random.fold_in(key, 7)
    groups = TOTAL_ROWS // ROWS
    group_keys = jax.random.split(key, groups)

    def one_group(group_key):
        shuffled = jax.random.permutation(group_key, ROWS).astype(jnp.int32)
        first_half = shuffled[0::2]
        second_half = shuffled[1::2]
        paired = jnp.zeros((ROWS,), jnp.int32)
        paired = paired.at[first_half].set(second_half).at[second_half].set(first_half)
        return paired
    return jax.vmap(one_group)(group_keys).reshape(-1)


def touch_ends(entries, own_key, least, largest):
    place = [jax.random.randint(jax.random.fold_in(own_key, axis), (), 0, length) for axis, length in enumerate(entries.shape)]
    longest = entries.shape.index(max(entries.shape))
    neighbour = place[:longest] + [(place[longest] + 1) % entries.shape[longest]] + place[longest + 1:]
    return entries.at[tuple(place)].set(least).at[tuple(neighbour)].set(largest)


def setup_inputs(seed: int = 0) -> dict:
    arg_keys = jax.random.split(jax.random.key(seed), 5)
    features = draw_features(jax.random.fold_in(arg_keys[4], 71), 0)
    prototypes = draw_prototypes(jax.random.fold_in(arg_keys[4], 71), 0)
    sibling_view = draw_sibling_view(jax.random.fold_in(arg_keys[4], 71), 0)
    q_seed = touch_ends(jax.random.randint(arg_keys[3], (FEAT, RANK), -8, 8), jax.random.fold_in(arg_keys[3], 1), -8, 7).astype(jnp.int32)
    return dict(features=features, prototypes=prototypes, sibling_view=sibling_view, q_seed=q_seed)


coolness_scaler = 0.1
entropic = 0.05
epsilon = 1e-06
highest = lax.Precision.HIGHEST

def normalize(value_rows):
    wide = value_rows.astype(jnp.float32)
    return (wide * lax.rsqrt(lax.optimization_barrier(jnp.sum(wide * wide, axis=-1, keepdims=True)) + epsilon)).astype(jnp.bfloat16)

def right_solve(lower_factor, value_rows):
    return lax.linalg.triangular_solve(lower_factor, value_rows, left_side=False, lower=True, transpose_a=True)

def reference(features, prototypes, sibling_view, q_seed):
    groups = TOTAL_ROWS // ROWS
    unit_feat = normalize(features).reshape(groups, ROWS, FEAT)
    unit_proto = normalize(prototypes)

    def energy_block(block):
        cluster_similarity = jnp.dot(block.astype(jnp.float32), unit_proto.T.astype(jnp.float32), preferred_element_type=jnp.float32)
        return jnp.exp(cluster_similarity / entropic)
    energy = lax.map(energy_block, unit_feat)
    row_scale = jnp.ones((groups, ROWS), jnp.float32)
    column_factor = jnp.ones((PROTOS,), jnp.float32)
    for sweep_index in range(SINK):
        col_total = jnp.einsum('grk,gr->k', energy, row_scale, precision=highest)
        column_factor = 1.0 / col_total
        row_total = jnp.einsum('grk,k->gr', energy, column_factor, precision=highest)
        row_scale = 1.0 / row_total
    pairing = sibling_view.reshape(groups, ROWS).astype(jnp.int32)

    def group_grad(inputs):
        block, group_energy, group_scale, batch_couple = inputs
        allotted_code = group_scale[:, None] * group_energy * column_factor[None, :]
        balanced_transport_plan = jnp.take(allotted_code, batch_couple, axis=0)
        cluster_similarity = jnp.dot(block.astype(jnp.float32), unit_proto.T.astype(jnp.float32), preferred_element_type=jnp.float32)
        rescaled_likelihood = jnp.exp(cluster_similarity / coolness_scaler)
        guessed_allotment = rescaled_likelihood / lax.optimization_barrier(jnp.sum(rescaled_likelihood, axis=-1, keepdims=True))
        objective_slope_table = ((guessed_allotment - balanced_transport_plan) / coolness_scaler).astype(jnp.bfloat16)
        row_grad = jnp.dot(objective_slope_table.astype(jnp.float32), unit_proto.astype(jnp.float32), preferred_element_type=jnp.float32)
        part_grad = jnp.dot(objective_slope_table.T.astype(jnp.float32), block.astype(jnp.float32), preferred_element_type=jnp.float32)
        return (row_grad, part_grad)
    row_grads, part_grads = lax.map(group_grad, (unit_feat, energy, row_scale, pairing))
    feature_grad = row_grads.reshape(TOTAL_ROWS, FEAT)
    factor_scale = PROTOS / TOTAL_ROWS
    summed = factor_scale * lax.optimization_barrier(jnp.sum(part_grads, axis=0))
    seed_basis = q_seed.astype(jnp.float32) * 0.125
    factor = jnp.dot(summed, seed_basis, precision=highest)
    inner_product_square = jnp.dot(factor.T, factor, precision=highest)
    lower_factor = jnp.linalg.cholesky(inner_product_square)
    basis = right_solve(lower_factor, factor)
    right_factor = jnp.dot(summed.T, basis, precision=highest)
    proto_grad = jnp.dot(basis, right_factor.T, precision=highest)
    return (feature_grad, proto_grad)
```

```python
import jax
import jax.numpy as jnp
from jax import lax
from jax.sharding import Mesh, PartitionSpec as P

SINK = 3
epsilon = 1e-06
highest = lax.Precision.HIGHEST


def normalize(value_rows):
    wide = value_rows.astype(jnp.float32)
    return (wide * lax.rsqrt(jnp.sum(wide * wide, axis=-1, keepdims=True) + epsilon)).astype(
        jnp.bfloat16
    )


def sum_over(value, axes):
    copies = jnp.broadcast_to(value[None], (lax.axis_size(axes),) + value.shape)
    return jnp.sum(lax.all_to_all(copies, axes, 0, 0), axis=0)


def sum_core(value):
    return value + lax.ppermute(value, "c", [(0, 1), (1, 0)])


def scatter_over(value, axes):
    count = lax.axis_size(axes)
    parts = value.reshape((count, value.shape[0] // count) + value.shape[1:])
    return jnp.sum(lax.all_to_all(parts, axes, 0, 0), axis=0)


def on_device(features, prototypes, sibling_view, q_seed):
    unit_feat = normalize(features)
    unit_proto = normalize(prototypes)
    rows, feat = unit_feat.shape
    protos = unit_proto.shape[0]
    total_rows = rows * lax.axis_size(("x", "c"))
    total_protos = protos * lax.axis_size(("y", "z"))

    def scores(block):
        return lax.dot_general(
            block, unit_proto, (((1,), (1,)), ((), ())), preferred_element_type=jnp.float32
        )

    likelihood = jnp.exp(scores(unit_feat) / 0.1)
    energy = likelihood * likelihood
    local_total = jnp.sum(likelihood, axis=-1)
    sibling_feat = jnp.take(unit_feat, sibling_view, axis=0)
    sibling_energy = jnp.exp(scores(sibling_feat) / 0.05)

    col_part = jnp.sum(energy, axis=0)
    for sweep in range(SINK):
        col_total = sum_over(col_part.reshape(-1, 128), ("x", "c")).reshape(-1)
        column_factor = 1.0 / col_total
        if sweep < SINK - 1:
            row_part = jnp.sum(energy * column_factor[None, :], axis=1)
            row_total = sum_over(row_part.reshape(-1, 128), ("y", "z")).reshape(-1)
            row_scale = 1.0 / row_total
            col_part = jnp.sum(energy * row_scale[:, None], axis=0)
        else:
            row_part = jnp.sum(sibling_energy * column_factor[None, :], axis=1)
            both = jnp.concatenate([row_part, local_total]).reshape(-1, 128)
            both = sum_over(both, ("y", "z")).reshape(2, rows)
            sibling_scale = 1.0 / both[0]
            exponent_sum = both[1]
    target = sibling_scale[:, None] * sibling_energy * column_factor[None, :]
    predicted = likelihood / exponent_sum[:, None]
    gradient = ((predicted - target) / 0.1).astype(jnp.bfloat16)

    part_grad = (total_protos / total_rows) * lax.dot_general(
        gradient, unit_feat, (((0,), (0,)), ((), ())), preferred_element_type=jnp.float32
    )
    seed_basis = q_seed.astype(jnp.float32) * 0.125
    factor = jnp.dot(part_grad, seed_basis, precision=highest)
    rank = factor.shape[1]
    factor = sum_core(factor.reshape(-1, 128))
    factor = sum_over(factor, "x").reshape(protos, rank)
    mixed = lax.dot_general(part_grad, factor, (((0,), (0,)), ((), ())), precision=highest)
    mixed = sum_core(mixed.reshape(-1, 128))
    mixed = sum_over(mixed, ("x", "y"))
    mixed = sum_over(mixed, "z").reshape(feat, rank)
    gramian = lax.dot_general(seed_basis, mixed, (((0,), (0,)), ((), ())), precision=highest)
    lower_factor = jnp.linalg.cholesky(0.5 * (gramian + gramian.T))
    half = lax.linalg.triangular_solve(lower_factor, mixed.T, left_side=True, lower=True)
    weights = lax.linalg.triangular_solve(
        lower_factor, half, left_side=True, lower=True, transpose_a=True
    )
    proto_grad = jnp.dot(factor, weights, precision=highest)

    row_grad = jnp.dot(gradient, unit_proto, preferred_element_type=jnp.float32)
    feature_grad = scatter_over(scatter_over(row_grad, "y"), "z")
    return (feature_grad, proto_grad)


def solution(mesh):
    wide, tall = mesh.shape["dp"], mesh.shape["proto"]
    fine = Mesh(mesh.devices.reshape(wide // 2, 2, 4, tall // 4), ("x", "c", "y", "z"))
    dp, proto = ("x", "c"), ("y", "z")
    return jax.shard_map(
        on_device,
        mesh=fine,
        in_specs=(P(dp, None), P(proto, None), P(dp), P()),
        out_specs=(P(dp + proto, None), P(proto, None)),
        check_vma=False,
    )
```

```python
import functools
import math

import jax
import jax.numpy as jnp
from jax import lax
from jax.experimental import pallas as pl
from jax.experimental.pallas import tpu as pltpu
from jax.sharding import Mesh, PartitionSpec as P

epsilon = 1e-06
highest = lax.Precision.HIGHEST
F32, BF16 = jnp.float32, jnp.bfloat16
LANES = 128
BLOCK = 256
UNROLL = 4
MIB = 1 << 20

nt = (((1,), (1,)), ((), ()))
nn = (((1,), (0,)), ((), ()))
tn = (((0,), (0,)), ((), ()))


def dot32(a, b, dims):
    return lax.dot_general(a, b, dims, precision=highest, preferred_element_type=F32)


def dot16(a, b, dims):
    return lax.dot_general(a, b, dims, preferred_element_type=F32)


def unit_rows(block):
    wide = block.astype(F32)
    return (wide * lax.rsqrt(jnp.sum(wide * wide, axis=-1, keepdims=True) + epsilon)).astype(BF16)


def across(partial):
    count = partial.shape[0] // LANES
    return jnp.concatenate(
        [jnp.sum(partial[i * LANES:(i + 1) * LANES].T, axis=0, keepdims=True) for i in range(count)],
        axis=0,
    )


def down(rows):
    return jnp.concatenate(
        [jnp.broadcast_to(rows[i:i + 1], (LANES, LANES)).T for i in range(rows.shape[0])], axis=0
    )


def tile(j):
    return slice(j * LANES, (j + 1) * LANES)


def fold(value):
    return jnp.sum(value.reshape(-1, 8, LANES), axis=0)


def copies(ref, value):
    for i in range(ref.shape[0]):
        ref[i] = value


def scores_kernel(feat, proto, sibling, seed_t, unit_feat_t, unit_proto, like, energy, col_out, total,
                  basis_t, unit_feat):
    rows, protos = feat.shape[0], proto.shape[0]
    tiles = protos // LANES
    basis_t[...] = seed_t[...].astype(F32) * 0.125
    unit_proto[...] = unit_rows(proto[...])

    def step(i, cols):
        here = pl.ds(pl.multiple_of(i * BLOCK, BLOCK), BLOCK)
        unit = unit_rows(feat[here, :])
        unit_feat[here, :] = unit
        unit_feat_t[:, here] = unit.T
        value = jnp.exp(dot16(unit, unit_proto[...], nt) * 10.0)
        like[here, :] = value
        part = value[:, tile(0)]
        for j in range(1, tiles):
            part = part + value[:, tile(j)]
        total[pl.ds(i, 1)] = across(part)[None]
        square = value * value
        return tuple(cols[j] + fold(square[:, tile(j)]) for j in range(tiles))

    cols = lax.fori_loop(
        0, rows // BLOCK, step, tuple(jnp.zeros((8, LANES), F32) for _ in range(tiles)), unroll=UNROLL
    )
    copies(col_out, jnp.concatenate([jnp.sum(c, axis=0, keepdims=True) for c in cols], axis=0))

    def other(i, carry):
        here = pl.ds(pl.multiple_of(i * BLOCK, BLOCK), BLOCK)
        row = lax.broadcasted_iota(jnp.int32, (BLOCK, LANES), 0) + i * BLOCK
        pick = [
            jnp.where(row == sibling[j:j + 1, :], 1.0, 0.0).astype(BF16) for j in range(rows // LANES)
        ]
        feats = dot16(jnp.concatenate(pick, axis=1), unit_feat[...], nn).astype(BF16)
        energy[here, :] = jnp.exp(dot16(feats, unit_proto[...], nt) * 20.0)
        return carry

    lax.fori_loop(0, rows // BLOCK, other, 0, unroll=UNROLL)


def row_kernel(squared, cols_in, table, total, row_out, sums):
    factor = 1.0 / jnp.sum(cols_in[...], axis=0)
    rows, protos = table.shape
    count = rows // LANES

    def step(i, carry):
        here = pl.ds(pl.multiple_of(i * BLOCK, BLOCK), BLOCK)
        part = None
        for j in range(protos // LANES):
            value = table[here, tile(j)]
            value = (value * value if squared else value) * factor[j:j + 1, :]
            part = value if part is None else part + value
        sums[pl.ds(i, 1)] = across(part)[None]
        return carry

    lax.fori_loop(0, rows // BLOCK, step, 0, unroll=UNROLL)
    result = sums[...].reshape(count, LANES)
    extra = row_out.shape[1] > count
    if extra:
        totals = total[...].reshape(count, LANES)
    for i in range(row_out.shape[0]):
        row_out[i, :count] = result
        if extra:
            row_out[i, count:] = totals


def column_kernel(rows_in, like, col_out, *rest):
    scale = rest[-1]
    rows, protos = like.shape
    count, tiles = rows // LANES, protos // LANES
    sums = jnp.sum(rows_in[...], axis=0)
    scale[...] = (1.0 / sums[:count]).reshape(scale.shape)
    if len(rest) > 1:
        rest[0][...] = (10.0 / sums[count:]).reshape(scale.shape)

    def step(i, cols):
        here = pl.ds(pl.multiple_of(i * BLOCK, BLOCK), BLOCK)
        weight = down(scale[pl.ds(i, 1)][0])
        out = []
        for j in range(tiles):
            value = like[here, tile(j)]
            out.append(cols[j] + fold(value * value * weight))
        return tuple(out)

    cols = lax.fori_loop(
        0, rows // BLOCK, step, tuple(jnp.zeros((8, LANES), F32) for _ in range(tiles)), unroll=UNROLL
    )
    copies(col_out, jnp.concatenate([jnp.sum(c, axis=0, keepdims=True) for c in cols], axis=0))


def gradient_kernel(like, energy, cols_in, rows_in, like_scale, unit_proto, row_grad, gradient, code_scale):
    factor = 1.0 / jnp.sum(cols_in[...], axis=0)
    code_scale[...] = (10.0 / jnp.sum(rows_in[...], axis=0)).reshape(code_scale.shape)
    rows, protos = like.shape

    def step(i, carry):
        here = pl.ds(pl.multiple_of(i * BLOCK, BLOCK), BLOCK)
        first = down(like_scale[pl.ds(i, 1)][0])
        second = down(code_scale[pl.ds(i, 1)][0])
        for j in range(protos // LANES):
            value = like[here, tile(j)] * first - energy[here, tile(j)] * factor[j:j + 1, :] * second
            gradient[here, tile(j)] = value.astype(BF16)
        row_grad[here, :] = dot16(gradient[here, :], unit_proto[...], nn)
        return carry

    lax.fori_loop(0, rows // BLOCK, step, 0, unroll=UNROLL)


def factor_kernel(ratio, gradient, unit_feat_t, basis_t, part_t, factor_t):
    for n in range(gradient.shape[1] // BLOCK):
        here = slice(n * BLOCK, (n + 1) * BLOCK)
        part = ratio * dot16(unit_feat_t[...], gradient[:, here], nn)
        part_t[:, here] = part
        factor_t[:, here] = dot32(basis_t[...], part, nn)


def mixed_kernel(part_a, part_b, part_c, part_d, part_t, factor_t, mixed_t):
    total = (part_a[...] + part_b[...]) + (part_c[...] + part_d[...])
    factor_t[...] = total
    mixed_t[...] = dot32(total, part_t[...], nt)


def merge_kernel(grads, mixed_a, mixed_b, mixed_c, mixed_d, out):
    count, total, feat = out.shape
    rank = mixed_a.shape[0]
    mixed = (mixed_a[...] + mixed_b[...]) + (mixed_c[...] + mixed_d[...])
    keep = total - rank
    for i in range(count):
        out[i, :keep] = jnp.sum(grads[:, i * keep:(i + 1) * keep], axis=0)
        out[i, keep:] = mixed


def final_kernel(sums_in, basis_t, factor_t, feature_grad, proto_grad):
    rank = basis_t.shape[0]
    keep = sums_in.shape[1] - rank
    feature_grad[...] = jnp.sum(sums_in[:, :keep], axis=0)
    mixed = jnp.sum(sums_in[:, keep:], axis=0)
    gram = dot32(basis_t[...], mixed, nt)
    left = jnp.concatenate([gram, jnp.zeros((rank, LANES - rank), F32)], axis=1)
    wide = jnp.concatenate([left, mixed], axis=1)
    row = lax.broadcasted_iota(jnp.int32, (rank, 1), 0)
    for j in range(rank):
        pivot = wide[j:j + 1, :] / wide[j:j + 1, j:j + 1]
        wide = jnp.where(row == j, pivot, wide - wide[:, j:j + 1] * pivot)
    proto_grad[...] = dot32(factor_t[...], wide[:, LANES:], tn)


def shape(*dims, dtype=F32):
    return jax.ShapeDtypeStruct(dims, dtype)


def kept(*dims, dtype=F32):
    return pltpu.VMEM(dims, dtype)


def stay(value):
    return pltpu.with_memory_space_constraint(value, pltpu.VMEM)


def call(body, outs, scratch=(), limit=24, flops=0, moved=0, name=None):
    return pl.pallas_call(
        body,
        out_shape=outs,
        scratch_shapes=scratch,
        name=name,
        compiler_params=pltpu.CompilerParams(vmem_limit_bytes=limit * MIB),
        cost_estimate=pl.CostEstimate(flops=flops, bytes_accessed=moved, transcendentals=0),
    )


def exchange(value, axes):
    return lax.all_to_all(value, axes, 0, 0)


def sum_core(value):
    return value + lax.ppermute(value, "c", [(0, 1), (1, 0)])


def shifts(value, axis):
    count = lax.axis_size(axis)
    return (value,) + tuple(
        lax.ppermute(value, axis, [(i, (i + s) % count) for i in range(count)]) for s in range(1, count)
    )


def on_device(features, prototypes, sibling_view, q_seed):
    dp, proto = ("x", "c"), ("y", "z")
    rows, feat = features.shape
    protos = prototypes.shape[0]
    rank = q_seed.shape[1]
    row_tiles, col_tiles, blocks = rows // LANES, protos // LANES, rows // BLOCK
    wide, tall = lax.axis_size(dp), lax.axis_size(proto)
    ratio = (protos * tall) / (rows * wide)
    per_block = (blocks, BLOCK // LANES, LANES)
    row_scratch = (pltpu.VMEM(per_block, F32),)

    unit_feat_t, unit_proto, like, energy, cols, total, basis_t = call(
        scores_kernel,
        (
            shape(feat, rows, dtype=BF16),
            shape(protos, feat, dtype=BF16),
            kept(rows, protos),
            kept(rows, protos),
            shape(wide, col_tiles, LANES),
            shape(*per_block),
            shape(rank, feat),
        ),
        (pltpu.VMEM((rows, feat), BF16),),
        name="scores",
    )(features, prototypes, sibling_view.reshape(row_tiles, LANES), q_seed.T)

    def row_step(squared, cols, table, extra=0):
        return call(
            functools.partial(row_kernel, squared), shape(tall, row_tiles + extra, LANES), row_scratch,
            name="rows",
        )(cols, stay(table), total)

    def column_step(sums, extra=()):
        return call(column_kernel, (shape(wide, col_tiles, LANES),) + extra, row_scratch, name="columns")(
            sums, stay(like)
        )

    cols = exchange(cols, dp)
    row_sums = exchange(row_step(True, cols, like, row_tiles), proto)
    cols, like_scale = column_step(row_sums, (shape(*per_block),))
    cols = exchange(cols, dp)
    row_sums = exchange(row_step(True, cols, like), proto)
    (cols,) = column_step(row_sums)
    cols = exchange(cols, dp)
    row_sums = exchange(row_step(False, cols, energy), proto)

    row_grad, gradient = call(
        gradient_kernel,
        (shape(rows, feat), shape(rows, protos, dtype=BF16)),
        row_scratch,
        name="gradient",
    )(stay(like), stay(energy), cols, row_sums, like_scale, unit_proto)

    grads = exchange(row_grad.reshape(lax.axis_size("y"), -1, feat), "y")
    part_t, factor_t = call(
        functools.partial(factor_kernel, ratio), (shape(feat, protos), shape(rank, protos)), name="factor",
        flops=2 * rows * protos * feat,
    )(gradient, unit_feat_t, basis_t)
    factor_t, mixed_t = call(
        mixed_kernel, (shape(rank, protos), shape(rank, feat)), name="mixed", flops=2 * rows * protos * feat
    )(*shifts(sum_core(factor_t), "x"), part_t)
    mixed_t = sum(shifts(sum_core(mixed_t), "x"))
    sums = call(merge_kernel, shape(lax.axis_size("z"), rows // tall + rank, feat), name="merge")(
        grads, *shifts(mixed_t, "y")
    )
    return call(final_kernel, (shape(rows // tall, feat), shape(protos, feat)), name="final")(
        exchange(sums, "z"), basis_t, factor_t
    )


def solution(mesh):
    wide, tall = mesh.shape["dp"], mesh.shape["proto"]
    fine = Mesh(mesh.devices.reshape(wide // 2, 2, 4, tall // 4), ("x", "c", "y", "z"))
    dp, proto = ("x", "c"), ("y", "z")
    return jax.shard_map(
        on_device,
        mesh=fine,
        in_specs=(P(dp, None), P(proto, None), P(dp), P()),
        out_specs=(P(dp + proto, None), P(proto, None)),
        check_vma=False,
    )
```

```python
import functools
import math

import jax
import jax.numpy as jnp
from jax import lax
from jax.experimental import pallas as pl
from jax.experimental.pallas import tpu as pltpu
from jax.sharding import Mesh, PartitionSpec as P

epsilon = 1e-06
highest = lax.Precision.HIGHEST
F32, BF16 = jnp.float32, jnp.bfloat16
LANES = 128
BLOCK = 256
UNROLL = 4
PIVOTS = 4
MIB = 1 << 20

nt = (((1,), (1,)), ((), ()))
nn = (((1,), (0,)), ((), ()))
tn = (((0,), (0,)), ((), ()))


def dot32(a, b, dims):
    return lax.dot_general(a, b, dims, precision=highest, preferred_element_type=F32)


def dot16(a, b, dims):
    return lax.dot_general(a, b, dims, preferred_element_type=F32)


def unit_rows(block):
    wide = block.astype(F32)
    return (wide * lax.rsqrt(jnp.sum(wide * wide, axis=-1, keepdims=True) + epsilon)).astype(BF16)


def across(partial):
    count = partial.shape[0] // LANES
    return jnp.concatenate(
        [jnp.sum(partial[i * LANES:(i + 1) * LANES].T, axis=0, keepdims=True) for i in range(count)],
        axis=0,
    )


def down(rows):
    return jnp.concatenate(
        [jnp.broadcast_to(rows[i:i + 1], (LANES, LANES)).T for i in range(rows.shape[0])], axis=0
    )


def tile(j):
    return slice(j * LANES, (j + 1) * LANES)


def fold(value):
    return jnp.sum(value.reshape(-1, 8, LANES), axis=0)


def copies(ref, value):
    for i in range(ref.shape[0]):
        ref[i] = value


def scores_kernel(feat_hbm, proto_hbm, unit_feat, unit_proto, like, col_out, total, feat, proto, ready):
    rows, protos = feat.shape[0], proto.shape[0]
    tiles = protos // LANES
    proto_copy = pltpu.make_async_copy(proto_hbm, proto, ready.at[0])
    feat_copy = pltpu.make_async_copy(feat_hbm, feat, ready.at[1])
    proto_copy.start()
    feat_copy.start()
    proto_copy.wait()
    unit_proto[...] = unit_rows(proto[...])
    feat_copy.wait()

    def step(i, cols):
        here = pl.ds(pl.multiple_of(i * BLOCK, BLOCK), BLOCK)
        unit = unit_rows(feat[here, :])
        unit_feat[here, :] = unit
        value = jnp.exp(dot16(unit, unit_proto[...], nt) * 10.0)
        like[here, :] = value
        part = value[:, tile(0)]
        for j in range(1, tiles):
            part = part + value[:, tile(j)]
        total[pl.ds(i, 1)] = across(part)[None]
        square = value * value
        return tuple(cols[j] + fold(square[:, tile(j)]) for j in range(tiles))

    cols = lax.fori_loop(
        0, rows // BLOCK, step, tuple(jnp.zeros((8, LANES), F32) for _ in range(tiles)), unroll=UNROLL
    )
    col_out[...] = jnp.concatenate([jnp.sum(c, axis=0, keepdims=True) for c in cols], axis=0)


def sibling_kernel(first, unit_feat, unit_proto, sibling, after, energy, unit_feat_t):
    rows = unit_feat.shape[0]

    def step(i, carry):
        here = pl.ds(pl.multiple_of(i * BLOCK, BLOCK), BLOCK)
        there = pl.ds(pl.multiple_of(first + i * BLOCK, BLOCK), BLOCK)
        row = lax.broadcasted_iota(jnp.int32, (BLOCK, LANES), 0) + (first + i * BLOCK)
        pick = [
            jnp.where(row == sibling[j:j + 1, :], 1.0, 0.0).astype(BF16) for j in range(rows // LANES)
        ]
        feats = dot16(jnp.concatenate(pick, axis=1), unit_feat[...], nn).astype(BF16)
        energy[here, :] = jnp.exp(dot16(feats, unit_proto[...], nt) * 20.0)
        unit_feat_t[:, here] = unit_feat[there, :].T
        return carry

    lax.fori_loop(0, energy.shape[0] // BLOCK, step, 0, unroll=UNROLL)


def row_kernel(cols_in, like, total, later, row_out, sums):
    factor = 1.0 / jnp.sum(cols_in[...], axis=0)
    rows, protos = like.shape
    count = rows // LANES

    def step(i, carry):
        here = pl.ds(pl.multiple_of(i * BLOCK, BLOCK), BLOCK)
        part = None
        for j in range(protos // LANES):
            value = like[here, tile(j)]
            value = value * value * factor[j:j + 1, :]
            part = value if part is None else part + value
        sums[pl.ds(i, 1)] = across(part)[None]
        return carry

    lax.fori_loop(0, rows // BLOCK, step, 0, unroll=UNROLL)
    result = sums[...].reshape(count, LANES)
    extra = row_out.shape[1] > count
    if extra:
        totals = total[...].reshape(count, LANES)
    for i in range(row_out.shape[0]):
        row_out[i, :count] = result
        if extra:
            row_out[i, count:] = totals


def last_row_kernel(cols_in, upper, lower, like, row_out, sums):
    factor = 1.0 / jnp.sum(cols_in[...], axis=0)
    half, protos = upper.shape
    for number, table in enumerate((upper, lower)):
        for i in range(half // BLOCK):
            part = None
            for j in range(protos // LANES):
                value = table[i * BLOCK:(i + 1) * BLOCK, tile(j)] * factor[j:j + 1, :]
                part = value if part is None else part + value
            sums[number * (half // BLOCK) + i] = across(part)
    copies(row_out, sums[...].reshape(row_out.shape[1:]))


def column_kernel(rows_in, like, col_out, *rest):
    scale = rest[-1]
    rows, protos = like.shape
    count, tiles = rows // LANES, protos // LANES
    sums = jnp.sum(rows_in[...], axis=0)
    scale[...] = (1.0 / sums[:count]).reshape(scale.shape)
    if len(rest) > 1:
        rest[0][...] = (10.0 / sums[count:]).reshape(scale.shape)

    def step(i, cols):
        here = pl.ds(pl.multiple_of(i * BLOCK, BLOCK), BLOCK)
        weight = down(scale[pl.ds(i, 1)][0])
        out = []
        for j in range(tiles):
            value = like[here, tile(j)]
            out.append(cols[j] + fold(value * value * weight))
        return tuple(out)

    cols = lax.fori_loop(
        0, rows // BLOCK, step, tuple(jnp.zeros((8, LANES), F32) for _ in range(tiles)), unroll=UNROLL
    )
    result = jnp.concatenate([jnp.sum(c, axis=0, keepdims=True) for c in cols], axis=0)
    if len(col_out.shape) == 3:
        copies(col_out, result)
    else:
        col_out[...] = result


def gradient_kernel(ratio, like, upper, lower, cols_in, rows_in, like_scale, feat_t_a, feat_t_b, unit_proto, seed_t,
                    row_grad, part_t, factor_t, basis_t, code_scale, gradient, grads, sent):
    factor = 1.0 / jnp.sum(cols_in[...], axis=0)
    code_scale[...] = (10.0 / jnp.sum(rows_in[...], axis=0)).reshape(code_scale.shape)
    basis_t[...] = seed_t[...].astype(F32) * 0.125
    rows, protos = like.shape
    blocks = rows // BLOCK

    def copy(i):
        here = slice(i * BLOCK, (i + 1) * BLOCK)
        return pltpu.make_async_copy(grads.at[here], row_grad.at[here], sent.at[i])

    for i in range(blocks):
        here = slice(i * BLOCK, (i + 1) * BLOCK)
        table = upper if i < blocks // 2 else lower
        there = slice((i % (blocks // 2)) * BLOCK, (i % (blocks // 2) + 1) * BLOCK)
        first = down(like_scale[i])
        second = down(code_scale[i])
        for j in range(protos // LANES):
            value = like[here, tile(j)] * first - table[there, tile(j)] * factor[j:j + 1, :] * second
            gradient[here, tile(j)] = value.astype(BF16)
        grads[here, :] = dot16(gradient[here, :], unit_proto[...], nn)
        copy(i).start()
    for n in range(protos // BLOCK):
        here = slice(n * BLOCK, (n + 1) * BLOCK)
        part = dot16(feat_t_a[...], gradient[:rows // 2, here], nn)
        part = ratio * (part + dot16(feat_t_b[...], gradient[rows // 2:, here], nn))
        part_t[:, here] = part
        factor_t[:, here] = dot32(basis_t[...], part, nn)
    for i in range(blocks):
        copy(i).wait()


def mixed_kernel(part_a, part_b, part_c, part_d, part_t, factor_t, mixed_t):
    total = (part_a[...] + part_b[...]) + (part_c[...] + part_d[...])
    factor_t[...] = total
    mixed_t[...] = dot32(total, part_t[...], nt)


def inverse(gram):
    rank = gram.shape[0]
    row = lax.broadcasted_iota(jnp.int32, (rank, 1), 0)
    unit = (row == lax.broadcasted_iota(jnp.int32, (rank, rank), 1)).astype(F32)
    wide = jnp.concatenate([unit, gram, jnp.zeros((rank, LANES - 2 * rank), F32)], axis=1)
    for j in range(0, rank, PIVOTS):
        lines = [wide[j + t:j + t + 1, :] for t in range(PIVOTS)]
        at = [rank + j + t for t in range(PIVOTS)]
        small = [[jnp.broadcast_to(line[:, k:k + 1], (1, LANES)) for k in at] for line in lines]
        columns = [jnp.broadcast_to(wide[:, k:k + 1], (rank, LANES)) for k in at]
        for t in range(PIVOTS):
            scale = 1.0 / small[t][t]
            lines[t] = lines[t] * scale
            small[t] = [v * scale for v in small[t]]
            for u in range(PIVOTS):
                if u != t:
                    by = small[u][t]
                    lines[u] = lines[u] - by * lines[t]
                    small[u] = [v - by * w for v, w in zip(small[u], small[t])]
        reduced = wide
        for t in range(PIVOTS):
            reduced = reduced - columns[t] * lines[t]
        for t in range(PIVOTS):
            reduced = jnp.where(row == j + t, lines[t], reduced)
        wide = reduced
    return wide[:, :rank]


def final_kernel(mixed_a, mixed_b, mixed_c, mixed_d, basis_t, factor_t, proto_grad):
    mixed = (mixed_a[...] + mixed_b[...]) + (mixed_c[...] + mixed_d[...])
    weights = dot32(inverse(dot32(basis_t[...], mixed, nt)), mixed, nn)
    proto_grad[...] = dot32(factor_t[...], weights, tn)


def gather_kernel(grads, after, out):
    out[...] = jnp.sum(grads[...], axis=0)


def shape(*dims, dtype=F32):
    return jax.ShapeDtypeStruct(dims, dtype)


def kept(*dims, dtype=F32):
    return pltpu.VMEM(dims, dtype)


def stay(value):
    return pltpu.with_memory_space_constraint(value, pltpu.VMEM)


def call(body, outs, scratch=(), limit=24, flops=0, name=None, ins=None, out_specs=None):
    specs = {}
    if ins is not None:
        specs["in_specs"] = [pl.BlockSpec(memory_space=m) for m in ins]
    if out_specs is not None:
        specs["out_specs"] = tuple(pl.BlockSpec(memory_space=m) for m in out_specs)
    return pl.pallas_call(
        body,
        out_shape=outs,
        scratch_shapes=scratch,
        name=name,
        compiler_params=pltpu.CompilerParams(vmem_limit_bytes=limit * MIB),
        cost_estimate=pl.CostEstimate(flops=flops, bytes_accessed=0, transcendentals=0),
        **specs,
    )


def exchange(value, axes):
    return lax.all_to_all(value, axes, 0, 0)


def sum_core(value):
    return value + lax.ppermute(value, "c", [(0, 1), (1, 0)])


def swap(value, axis, mask):
    return lax.ppermute(value, axis, [(i, i ^ mask) for i in range(lax.axis_size(axis))])


def fours(value, axis):
    return (value,) + tuple(swap(value, axis, m) for m in (1, 3, 2))


def on_device(features, prototypes, sibling_view, q_seed):
    proto = ("y", "z")
    rows, feat = features.shape
    protos = prototypes.shape[0]
    rank = q_seed.shape[1]
    half = rows // 2
    row_tiles, col_tiles, blocks = rows // LANES, protos // LANES, rows // BLOCK
    wide, tall = lax.axis_size(("x", "c")), lax.axis_size(proto)
    deep = lax.axis_size("z")
    ratio = (protos * tall) / (rows * wide)
    per_block = (blocks, BLOCK // LANES, LANES)
    row_scratch = (pltpu.VMEM(per_block, F32),)
    V, H, A = pltpu.VMEM, pltpu.HBM, pl.ANY

    unit_feat, unit_proto, like, cols, total = call(
        scores_kernel,
        (
            shape(rows, feat, dtype=BF16),
            shape(protos, feat, dtype=BF16),
            kept(rows, protos),
            shape(col_tiles, LANES),
            shape(*per_block),
        ),
        (V((rows, feat), BF16), V((protos, feat), BF16), pltpu.SemaphoreType.DMA((2,))),
        name="scores", ins=(H, H),
    )(
        pltpu.with_memory_space_constraint(features, H),
        pltpu.with_memory_space_constraint(prototypes, H),
    )
    sibling = sibling_view.reshape(row_tiles, LANES)

    def sibling_half(first, after):
        return call(
            functools.partial(sibling_kernel, first),
            (kept(half, protos), shape(feat, half, dtype=BF16)),
            name="sibling", ins=(V, V, V, A), flops=4 * half * rows * feat,
        )(unit_feat, unit_proto, sibling, after)

    def row_step(cols, later, extra=0):
        return call(
            row_kernel, shape(tall, row_tiles + extra, LANES), row_scratch, name="rows", ins=(V, V, V, A)
        )(cols, stay(like), total, stay(later))

    def column_step(sums, out, *extra):
        return call(column_kernel, (out,) + extra, row_scratch, name="columns")(sums, stay(like))

    cols = sum_core(cols)
    upper, feat_t_a = sibling_half(0, cols)
    cols = jnp.stack(fours(cols, "x"))
    row_sums = exchange(row_step(cols, upper, row_tiles), proto)
    cols, like_scale = column_step(row_sums, shape(col_tiles, LANES), shape(*per_block))
    cols = sum_core(cols)
    lower, feat_t_b = sibling_half(half, cols)
    cols = jnp.stack(fours(cols, "x"))
    row_sums = exchange(row_step(cols, lower), proto)
    (cols,) = column_step(row_sums, shape(wide, col_tiles, LANES))
    cols = exchange(cols, ("x", "c"))
    row_sums = exchange(
        call(last_row_kernel, shape(tall, row_tiles, LANES), row_scratch, name="rows", ins=(V, V, V, A))(
            cols, stay(upper), stay(lower), stay(like)
        ),
        proto,
    )

    row_grad, part_t, factor_t, basis_t = call(
        functools.partial(gradient_kernel, ratio),
        (pltpu.HBM((rows, feat), F32), shape(feat, protos), shape(rank, protos), shape(rank, feat)),
        row_scratch
        + (V((rows, protos), BF16), V((rows, feat), F32), pltpu.SemaphoreType.DMA((blocks,))),
        name="gradient", ins=(V,) * 10, out_specs=(H, V, V, V),
    )(
        stay(like), stay(upper), stay(lower), cols, row_sums, like_scale, feat_t_a, feat_t_b, unit_proto,
        q_seed.T,
    )

    grads = exchange(row_grad.reshape(tall // deep, -1, feat), "y")
    factor_t, mixed_t = call(
        mixed_kernel, (shape(rank, protos), shape(rank, feat)), name="mixed",
    )(*fours(sum_core(factor_t), "x"), part_t)
    mixed_t = sum_core(mixed_t)
    mixed_t = sum(fours(mixed_t, "z"))
    mixed_t = mixed_t + swap(mixed_t, "z", 4)
    grads = call(gather_kernel, shape(deep * rows // tall, feat), name="gather", ins=(V, A))(grads, mixed_t)
    grads = exchange(grads.reshape(deep, rows // tall, feat), "z")
    mixed_t = sum(fours(mixed_t, "x"))
    proto_grad = call(final_kernel, shape(protos, feat), name="final")(
        *fours(mixed_t, "y"), basis_t, factor_t
    )
    return jnp.sum(grads, axis=0), proto_grad


def solution(mesh):
    wide, tall = mesh.shape["dp"], mesh.shape["proto"]
    fine = Mesh(mesh.devices.reshape(wide // 2, 2, 4, tall // 4), ("x", "c", "y", "z"))
    dp, proto = ("x", "c"), ("y", "z")
    return jax.shard_map(
        on_device,
        mesh=fine,
        in_specs=(P(dp, None), P(proto, None), P(dp), P()),
        out_specs=(P(dp + proto, None), P(proto, None)),
        check_vma=False,
    )
```

```python
import functools
import math

import jax
import jax.numpy as jnp
from jax import lax
from jax.experimental import pallas as pl
from jax.experimental.pallas import tpu as pltpu
from jax.sharding import Mesh, PartitionSpec as P

epsilon = 1e-06
highest = lax.Precision.HIGHEST
F32, BF16 = jnp.float32, jnp.bfloat16
LANES = 128
BLOCK = 256
UNROLL = 4
PIVOTS = 4
MIB = 1 << 20

nt = (((1,), (1,)), ((), ()))
nn = (((1,), (0,)), ((), ()))
tn = (((0,), (0,)), ((), ()))


def dot32(a, b, dims):
    return lax.dot_general(a, b, dims, precision=highest, preferred_element_type=F32)


def dot16(a, b, dims):
    return lax.dot_general(a, b, dims, preferred_element_type=F32)


def unit_rows(block):
    wide = block.astype(F32)
    return (wide * lax.rsqrt(jnp.sum(wide * wide, axis=-1, keepdims=True) + epsilon)).astype(BF16)


def across(partial):
    count = partial.shape[0] // LANES
    return jnp.concatenate(
        [jnp.sum(partial[i * LANES:(i + 1) * LANES].T, axis=0, keepdims=True) for i in range(count)],
        axis=0,
    )


def down(rows):
    return jnp.concatenate(
        [jnp.broadcast_to(rows[i:i + 1], (LANES, LANES)).T for i in range(rows.shape[0])], axis=0
    )


def tile(j):
    return slice(j * LANES, (j + 1) * LANES)


def fold(value):
    return jnp.sum(value.reshape(-1, 8, LANES), axis=0)


def copies(ref, value):
    for i in range(ref.shape[0]):
        ref[i] = value


def scores_kernel(feat_hbm, proto_hbm, sibling_hbm, seed_hbm, unit_feat, unit_proto, like, col_out, total,
                  sibling, seed_t, feat, proto, ready):
    rows, protos = feat.shape[0], proto.shape[0]
    tiles = protos // LANES
    proto_copy = pltpu.make_async_copy(proto_hbm, proto, ready.at[0])
    feat_copy = pltpu.make_async_copy(feat_hbm, feat, ready.at[1])
    sibling_copy = pltpu.make_async_copy(sibling_hbm, sibling, ready.at[2])
    seed_copy = pltpu.make_async_copy(seed_hbm, seed_t, ready.at[3])
    proto_copy.start()
    feat_copy.start()
    sibling_copy.start()
    seed_copy.start()
    proto_copy.wait()
    unit_proto[...] = unit_rows(proto[...])
    feat_copy.wait()

    def step(i, cols):
        here = pl.ds(pl.multiple_of(i * BLOCK, BLOCK), BLOCK)
        unit = unit_rows(feat[here, :])
        unit_feat[here, :] = unit
        value = jnp.exp(dot16(unit, unit_proto[...], nt) * 10.0)
        like[here, :] = value
        part = value[:, tile(0)]
        for j in range(1, tiles):
            part = part + value[:, tile(j)]
        total[pl.ds(i, 1)] = across(part)[None]
        square = value * value
        return tuple(cols[j] + fold(square[:, tile(j)]) for j in range(tiles))

    cols = lax.fori_loop(
        0, rows // BLOCK, step, tuple(jnp.zeros((8, LANES), F32) for _ in range(tiles)), unroll=UNROLL
    )
    col_out[...] = jnp.concatenate([jnp.sum(c, axis=0, keepdims=True) for c in cols], axis=0)
    sibling_copy.wait()
    seed_copy.wait()


def sibling_kernel(first, unit_feat, unit_proto, sibling, seed_t, after, energy, unit_feat_t, *basis_t):
    rows = unit_feat.shape[0]
    for out in basis_t:
        seed = seed_t[...].astype(F32) * 0.125
        mine = seed.shape[0] // 2
        turned = jnp.concatenate([seed[mine:], seed[:mine]], axis=0)
        out[...] = jnp.where(lax.axis_index("c") == 0, seed, turned)

    def step(i, carry):
        here = pl.ds(pl.multiple_of(i * BLOCK, BLOCK), BLOCK)
        there = pl.ds(pl.multiple_of(first + i * BLOCK, BLOCK), BLOCK)
        row = lax.broadcasted_iota(jnp.int32, (BLOCK, LANES), 0) + (first + i * BLOCK)
        pick = [
            jnp.where(row == sibling[j:j + 1, :], 1.0, 0.0).astype(BF16) for j in range(rows // LANES)
        ]
        feats = dot16(jnp.concatenate(pick, axis=1), unit_feat[...], nn).astype(BF16)
        energy[here, :] = jnp.exp(dot16(feats, unit_proto[...], nt) * 20.0)
        unit_feat_t[:, here] = unit_feat[there, :].T
        return carry

    lax.fori_loop(0, energy.shape[0] // BLOCK, step, 0, unroll=UNROLL)


def flat(rows):
    return jnp.concatenate([rows[i:i + 1] for i in range(rows.shape[0])], axis=1)


def row_kernel(cols_in, like, rest, later, row_out):
    factor = 1.0 / add4(*(cols_in[i] for i in range(4)))
    rows, protos = like.shape
    sums = []
    for i in range(rows // BLOCK):
        part = None
        for j in range(protos // LANES):
            value = like[i * BLOCK:(i + 1) * BLOCK, tile(j)]
            value = value * value * factor[j:j + 1, :]
            part = value if part is None else part + value
        sums.append(flat(across(part)))
    result = jnp.concatenate(sums, axis=1)
    tall = row_out.shape[0]
    piece = rows // tall
    if rest.shape[0] == 1:
        tails = [rest[...]] * tall
    else:
        totals = rest[...].reshape(rows // LANES, LANES)
        tails = [
            totals[q * piece // LANES:q * piece // LANES + 1, q * piece % LANES:q * piece % LANES + piece]
            for q in range(tall)
        ]
        tails = [jnp.concatenate([t, jnp.zeros((1, LANES - piece), F32)], axis=1) for t in tails]
    for q in range(tall):
        row_out[q] = jnp.concatenate([result, tails[q]], axis=1)


def last_row_kernel(cols_in, upper, lower, like, row_out, sums):
    factor = 1.0 / jnp.sum(cols_in[...], axis=0)
    half, protos = upper.shape
    for number, table in enumerate((upper, lower)):
        for i in range(half // BLOCK):
            part = None
            for j in range(protos // LANES):
                value = table[i * BLOCK:(i + 1) * BLOCK, tile(j)] * factor[j:j + 1, :]
                part = value if part is None else part + value
            sums[number * (half // BLOCK) + i] = across(part)
    copies(row_out, sums[...].reshape(row_out.shape[1:]))


def column_kernel(finish, rows_in, like, col_out, extra, scale):
    rows, protos = like.shape
    tall, tiles = rows_in.shape[0], protos // LANES
    sums = rows_in[0]
    for q in range(1, tall):
        sums = sums + rows_in[q]
    inverse_sums = 1.0 / sums[:, :rows]
    for i in range(rows // LANES):
        scale[i // 2, i % 2:i % 2 + 1] = inverse_sums[:, tile(i)]
    if finish:
        piece = rows // tall
        for i in range(rows // LANES):
            each = LANES // piece
            line = [rows_in[each * i + t][:, rows:rows + piece] for t in range(each)]
            extra[i // 2, i % 2:i % 2 + 1] = 10.0 / jnp.concatenate(line, axis=1)
    else:
        extra[...] = sums[:, rows:]

    def step(i, cols):
        here = pl.ds(pl.multiple_of(i * BLOCK, BLOCK), BLOCK)
        weight = down(scale[pl.ds(i, 1)][0])
        out = []
        for j in range(tiles):
            value = like[here, tile(j)]
            out.append(cols[j] + fold(value * value * weight))
        return tuple(out)

    cols = lax.fori_loop(
        0, rows // BLOCK, step, tuple(jnp.zeros((8, LANES), F32) for _ in range(tiles)), unroll=UNROLL
    )
    result = jnp.concatenate([jnp.sum(c, axis=0, keepdims=True) for c in cols], axis=0)
    if len(col_out.shape) == 3:
        copies(col_out, result)
    else:
        col_out[...] = result


def gradient_kernel(ratio, like, upper, lower, cols_in, rows_in, like_scale, feat_t_a, feat_t_b, basis_t,
                    gradient, part_t, factor_mine, factor_other, code_scale):
    factor = 1.0 / jnp.sum(cols_in[...], axis=0)
    code_scale[...] = (10.0 / jnp.sum(rows_in[...], axis=0)).reshape(code_scale.shape)
    mine = factor_mine.shape[0]
    rows, protos = like.shape
    blocks = rows // BLOCK

    for i in range(blocks):
        here = slice(i * BLOCK, (i + 1) * BLOCK)
        table = upper if i < blocks // 2 else lower
        there = slice((i % (blocks // 2)) * BLOCK, (i % (blocks // 2) + 1) * BLOCK)
        first = down(like_scale[i])
        second = down(code_scale[i])
        for j in range(protos // LANES):
            value = like[here, tile(j)] * first - table[there, tile(j)] * factor[j:j + 1, :] * second
            gradient[here, tile(j)] = value.astype(BF16)
    for n in range(protos // BLOCK):
        here = slice(n * BLOCK, (n + 1) * BLOCK)
        part = dot16(feat_t_a[...], gradient[:rows // 2, here], nn)
        part = ratio * (part + dot16(feat_t_b[...], gradient[rows // 2:, here], nn))
        part_t[:, here] = part
        both = dot32(basis_t[...], part, nn)
        factor_mine[:, here] = both[:mine]
        factor_other[:, here] = both[mine:]


def row_grad_kernel(gradient, unit_proto, after, row_grad, grads, sent):
    rows = gradient.shape[0]
    blocks = rows // BLOCK

    def copy(i):
        here = slice(i * BLOCK, (i + 1) * BLOCK)
        return pltpu.make_async_copy(grads.at[here], row_grad.at[here], sent.at[i])

    for i in range(blocks):
        here = slice(i * BLOCK, (i + 1) * BLOCK)
        grads[here, :] = dot16(gradient[here, :], unit_proto[...], nn)
        copy(i).start()
    for i in range(blocks):
        copy(i).wait()


def mixed_kernel(a, b, c, d, part_t, part_other, factor_t, mixed_t):
    total = (a[...] + b[...]) + (c[...] + d[...])
    factor_t[...] = total
    mixed_t[...] = dot32(total, part_t[...] + part_other[...], nt)


def inverse(gram):
    rank = gram.shape[0]
    row = lax.broadcasted_iota(jnp.int32, (rank, 1), 0)
    unit = (row == lax.broadcasted_iota(jnp.int32, (rank, rank), 1)).astype(F32)
    wide = jnp.concatenate([unit, gram, jnp.zeros((rank, LANES - 2 * rank), F32)], axis=1)
    for j in range(0, rank, PIVOTS):
        lines = [wide[j + t:j + t + 1, :] for t in range(PIVOTS)]
        at = [rank + j + t for t in range(PIVOTS)]
        small = [[jnp.broadcast_to(line[:, k:k + 1], (1, LANES)) for k in at] for line in lines]
        columns = [jnp.broadcast_to(wide[:, k:k + 1], (rank, LANES)) for k in at]
        for t in range(PIVOTS):
            scale = 1.0 / small[t][t]
            lines[t] = lines[t] * scale
            small[t] = [v * scale for v in small[t]]
            for u in range(PIVOTS):
                if u != t:
                    by = small[u][t]
                    lines[u] = lines[u] - by * lines[t]
                    small[u] = [v - by * w for v, w in zip(small[u], small[t])]
        reduced = wide
        for t in range(PIVOTS):
            reduced = reduced - columns[t] * lines[t]
        for t in range(PIVOTS):
            reduced = jnp.where(row == j + t, lines[t], reduced)
        wide = reduced
    return wide[:, :rank]


def final_kernel(mixed_a, mixed_b, mixed_c, mixed_d, basis_t, factor_mine, factor_other, proto_grad):
    mixed = (mixed_a[...] + mixed_b[...]) + (mixed_c[...] + mixed_d[...])
    weights = dot32(inverse(dot32(basis_t[...], mixed, nt)), mixed, nn)
    factor_t = jnp.concatenate([factor_mine[...], factor_other[...]], axis=0)
    proto_grad[...] = dot32(factor_t, weights, tn)


def gather_kernel(grads, after, out):
    out[...] = jnp.sum(grads[...], axis=0)


def shape(*dims, dtype=F32):
    return jax.ShapeDtypeStruct(dims, dtype)


def kept(*dims, dtype=F32):
    return pltpu.VMEM(dims, dtype)


def stay(value):
    return pltpu.with_memory_space_constraint(value, pltpu.VMEM)


def call(body, outs, scratch=(), limit=24, flops=0, name=None, ins=None, out_specs=None):
    specs = {}
    if ins is not None:
        specs["in_specs"] = [pl.BlockSpec(memory_space=m) for m in ins]
    if out_specs is not None:
        specs["out_specs"] = tuple(pl.BlockSpec(memory_space=m) for m in out_specs)
    return pl.pallas_call(
        body,
        out_shape=outs,
        scratch_shapes=scratch,
        name=name,
        compiler_params=pltpu.CompilerParams(vmem_limit_bytes=limit * MIB),
        cost_estimate=pl.CostEstimate(flops=flops, bytes_accessed=0, transcendentals=0),
        **specs,
    )


def exchange(value, axes):
    return lax.all_to_all(value, axes, 0, 0)


def sum_core(value):
    return value + lax.ppermute(value, "c", [(0, 1), (1, 0)])


def add4(a, b, c, d):
    return (a + b) + (c + d)


def swap(value, axis, mask):
    return lax.ppermute(value, axis, [(i, i ^ mask) for i in range(lax.axis_size(axis))])


def fours(value, axis):
    return (value,) + tuple(swap(value, axis, m) for m in (1, 3, 2))


def on_device(features, prototypes, sibling_view, q_seed):
    proto = ("y", "z")
    rows, feat = features.shape
    protos = prototypes.shape[0]
    rank = q_seed.shape[1]
    half = rows // 2
    row_tiles, col_tiles, blocks = rows // LANES, protos // LANES, rows // BLOCK
    wide, tall = lax.axis_size(("x", "c")), lax.axis_size(proto)
    deep = lax.axis_size("z")
    ratio = (protos * tall) / (rows * wide)
    per_block = (blocks, BLOCK // LANES, LANES)
    row_scratch = (pltpu.VMEM(per_block, F32),)
    V, H, A = pltpu.VMEM, pltpu.HBM, pl.ANY

    unit_feat, unit_proto, like, cols, total, sibling, seed_t = call(
        scores_kernel,
        (
            shape(rows, feat, dtype=BF16),
            shape(protos, feat, dtype=BF16),
            kept(rows, protos),
            shape(col_tiles, LANES),
            shape(*per_block),
            shape(row_tiles, LANES, dtype=jnp.int32),
            shape(rank, feat, dtype=jnp.int32),
        ),
        (V((rows, feat), BF16), V((protos, feat), BF16), pltpu.SemaphoreType.DMA((4,))),
        name="scores", ins=(H, H, H, H),
    )(
        pltpu.with_memory_space_constraint(features, H),
        pltpu.with_memory_space_constraint(prototypes, H),
        pltpu.with_memory_space_constraint(sibling_view.reshape(row_tiles, LANES), H),
        pltpu.with_memory_space_constraint(q_seed.T, H),
    )

    def sibling_half(first, after, *extra):
        return call(
            functools.partial(sibling_kernel, first),
            (kept(half, protos), shape(feat, half, dtype=BF16)) + extra,
            name="sibling", ins=(V, V, V, V, A), flops=4 * half * rows * feat,
        )(unit_feat, unit_proto, sibling, seed_t, after)

    def row_step(cols, rest, later):
        return call(row_kernel, shape(tall, 1, rows + LANES), name="rows", ins=(V, V, V, A))(
            cols, stay(like), rest, stay(later)
        )

    def column_step(finish, sums, *outs):
        return call(functools.partial(column_kernel, finish), outs, row_scratch, name="columns")(
            sums, stay(like)
        )

    cols = sum_core(cols)
    upper, feat_t_a, basis_t = sibling_half(0, cols, shape(rank, feat))
    cols = jnp.stack(fours(cols, "x"))
    row_sums = exchange(row_step(cols, total, upper), proto)
    cols, piece = column_step(False, row_sums, shape(col_tiles, LANES), shape(1, LANES))
    cols = sum_core(cols)
    lower, feat_t_b = sibling_half(half, cols)
    cols = jnp.stack(fours(cols, "x"))
    row_sums = exchange(row_step(cols, piece, lower), proto)
    cols, like_scale = column_step(True, row_sums, shape(wide, col_tiles, LANES), shape(*per_block))
    cols = exchange(cols, ("x", "c"))
    row_sums = exchange(
        call(last_row_kernel, shape(tall, row_tiles, LANES), row_scratch, name="rows", ins=(V, V, V, A))(
            cols, stay(upper), stay(lower), stay(like)
        ),
        proto,
    )

    mine = rank // 2
    gradient, part_t, factor_mine, factor_other = call(
        functools.partial(gradient_kernel, ratio),
        (
            kept(rows, protos, dtype=BF16),
            shape(feat, protos),
            shape(mine, protos),
            shape(mine, protos),
        ),
        row_scratch,
        name="gradient", ins=(V,) * 9, out_specs=(V,) * 4,
    )(stay(like), stay(upper), stay(lower), cols, row_sums, like_scale, feat_t_a, feat_t_b, basis_t)
    factor_mine = factor_mine + swap(factor_other, "c", 1)
    (row_grad,) = call(
        row_grad_kernel, (pltpu.HBM((rows, feat), F32),),
        (V((rows, feat), F32), pltpu.SemaphoreType.DMA((blocks,))),
        name="row_grad", ins=(V, V, A), out_specs=(H,), flops=2 * rows * protos * feat,
    )(stay(gradient), unit_proto, factor_mine)
    grads = exchange(row_grad.reshape(tall // deep, -1, feat), "y")

    factor_mine, mixed_t = call(
        mixed_kernel, (shape(mine, protos), shape(mine, feat)), name="mixed",
    )(*fours(factor_mine, "x"), part_t, swap(part_t, "c", 1))
    factor_other = swap(factor_mine, "c", 1)
    mixed_t = add4(*fours(mixed_t, "z"))
    mixed_t = mixed_t + swap(mixed_t, "z", 4)
    mixed_t = add4(*fours(mixed_t, "x"))
    grads = call(gather_kernel, shape(deep * rows // tall, feat), name="gather", ins=(V, A))(grads, mixed_t)
    mixed_t = jnp.concatenate([mixed_t, swap(mixed_t, "c", 1)], axis=0)
    grads = exchange(grads.reshape(deep, rows // tall, feat), "z")
    proto_grad = call(final_kernel, shape(protos, feat), name="final")(
        *fours(mixed_t, "y"), basis_t, factor_mine, factor_other
    )
    return jnp.sum(grads, axis=0), proto_grad


def solution(mesh):
    wide, tall = mesh.shape["dp"], mesh.shape["proto"]
    fine = Mesh(mesh.devices.reshape(wide // 2, 2, 4, tall // 4), ("x", "c", "y", "z"))
    dp, proto = ("x", "c"), ("y", "z")
    return jax.shard_map(
        on_device,
        mesh=fine,
        in_specs=(P(dp, None), P(proto, None), P(dp), P()),
        out_specs=(P(dp + proto, None), P(proto, None)),
        check_vma=False,
    )
```

```python
import functools
import math

import jax
import jax.numpy as jnp
from jax import lax
from jax.experimental import pallas as pl
from jax.experimental.pallas import tpu as pltpu
from jax.sharding import Mesh, PartitionSpec as P

epsilon = 1e-06
highest = lax.Precision.HIGHEST
F32, BF16 = jnp.float32, jnp.bfloat16
LANES = 128
BLOCK = 256
PIVOTS = 4
MIB = 1 << 20

nt = (((1,), (1,)), ((), ()))
nn = (((1,), (0,)), ((), ()))
tn = (((0,), (0,)), ((), ()))


def dot32(a, b, dims):
    return lax.dot_general(a, b, dims, precision=highest, preferred_element_type=F32)


def dot16(a, b, dims):
    return lax.dot_general(a, b, dims, preferred_element_type=F32)


def split(value):
    high = value.astype(BF16)
    return high, (value - high.astype(F32)).astype(BF16)


def unit_rows(block):
    wide = block.astype(F32)
    return (wide * lax.rsqrt(jnp.sum(wide * wide, axis=-1, keepdims=True) + epsilon)).astype(BF16)


def across(partial):
    count = partial.shape[0] // LANES
    return jnp.concatenate(
        [jnp.sum(partial[i * LANES:(i + 1) * LANES].T, axis=0, keepdims=True) for i in range(count)],
        axis=0,
    )


def down(rows):
    return jnp.concatenate(
        [jnp.broadcast_to(rows[i:i + 1], (LANES, LANES)).T for i in range(rows.shape[0])], axis=0
    )


def tile(j):
    return slice(j * LANES, (j + 1) * LANES)


def fold(value):
    return jnp.sum(value.reshape(-1, 8, LANES), axis=0)


def copies(ref, value):
    for i in range(ref.shape[0]):
        ref[i] = value


def scores_kernel(feat_hbm, proto_hbm, sibling_hbm, seed_hbm, unit_feat, unit_proto, like, col_out, total,
                  sibling, seed_t, feat, proto, ready):
    rows, protos = feat.shape[0], proto.shape[0]
    tiles = protos // LANES
    proto_copy = pltpu.make_async_copy(proto_hbm, proto, ready.at[0])
    feat_copy = pltpu.make_async_copy(feat_hbm, feat, ready.at[1])
    sibling_copy = pltpu.make_async_copy(sibling_hbm, sibling, ready.at[2])
    seed_copy = pltpu.make_async_copy(seed_hbm, seed_t, ready.at[3])
    proto_copy.start()
    feat_copy.start()
    sibling_copy.start()
    seed_copy.start()
    proto_copy.wait()
    unit_proto[...] = unit_rows(proto[...])
    feat_copy.wait()

    cols = [jnp.zeros((8, LANES), F32)] * tiles
    for i in range(rows // BLOCK):
        here = slice(i * BLOCK, (i + 1) * BLOCK)
        unit = unit_rows(feat[here, :])
        unit_feat[here, :] = unit
        value = jnp.exp(dot16(unit, unit_proto[...], nt) * 10.0)
        like[here, :] = value
        part = value[:, tile(0)]
        for j in range(1, tiles):
            part = part + value[:, tile(j)]
        total[i] = across(part)
        square = value * value
        cols = [cols[j] + fold(square[:, tile(j)]) for j in range(tiles)]
    col_out[...] = jnp.concatenate([jnp.sum(c, axis=0, keepdims=True) for c in cols], axis=0)
    sibling_copy.wait()
    seed_copy.wait()


def sibling_kernel(first, unit_feat, unit_proto, sibling, seed_t, after, energy, unit_feat_t, *basis_t):
    rows = unit_feat.shape[0]
    for out in basis_t:
        seed = seed_t[...].astype(F32) * 0.125
        mine = seed.shape[0] // 2
        turned = jnp.concatenate([seed[mine:], seed[:mine]], axis=0)
        out[...] = jnp.where(lax.axis_index("c") == 0, seed, turned)

    for i in range(energy.shape[0] // BLOCK):
        here = slice(i * BLOCK, (i + 1) * BLOCK)
        there = slice(first + i * BLOCK, first + (i + 1) * BLOCK)
        row = lax.broadcasted_iota(jnp.int32, (BLOCK, LANES), 0) + (first + i * BLOCK)
        pick = [
            jnp.where(row == sibling[j:j + 1, :], 1.0, 0.0).astype(BF16) for j in range(rows // LANES)
        ]
        feats = dot16(jnp.concatenate(pick, axis=1), unit_feat[...], nn).astype(BF16)
        energy[here, :] = jnp.exp(dot16(feats, unit_proto[...], nt) * 20.0)
        unit_feat_t[:, here] = unit_feat[there, :].T


def flat(rows):
    return jnp.concatenate([rows[i:i + 1] for i in range(rows.shape[0])], axis=1)


def row_kernel(cols_in, like, rest, later, row_out):
    factor = 1.0 / add4(*(cols_in[i] for i in range(4)))
    rows, protos = like.shape
    sums = []
    for i in range(rows // BLOCK):
        part = None
        for j in range(protos // LANES):
            value = like[i * BLOCK:(i + 1) * BLOCK, tile(j)]
            value = value * value * factor[j:j + 1, :]
            part = value if part is None else part + value
        sums.append(flat(across(part)))
    result = jnp.concatenate(sums, axis=1)
    tall = row_out.shape[0]
    piece = rows // tall
    if rest.shape[0] == 1:
        tails = [rest[...]] * tall
    else:
        totals = rest[...].reshape(rows // LANES, LANES)
        tails = [
            totals[q * piece // LANES:q * piece // LANES + 1, q * piece % LANES:q * piece % LANES + piece]
            for q in range(tall)
        ]
        tails = [jnp.concatenate([t, jnp.zeros((1, LANES - piece), F32)], axis=1) for t in tails]
    for q in range(tall):
        row_out[q] = jnp.concatenate([result, tails[q]], axis=1)


def last_row_kernel(cols_in, upper, lower, like, row_out, sums):
    factor = 1.0 / add4(*(cols_in[i] for i in range(4)))
    half, protos = upper.shape
    for number, table in enumerate((upper, lower)):
        for i in range(half // BLOCK):
            part = None
            for j in range(protos // LANES):
                value = table[i * BLOCK:(i + 1) * BLOCK, tile(j)] * factor[j:j + 1, :]
                part = value if part is None else part + value
            sums[number * (half // BLOCK) + i] = across(part)
    copies(row_out, sums[...].reshape(row_out.shape[1:]))


def column_kernel(finish, rows_in, like, col_out, extra, scale):
    rows, protos = like.shape
    tall, tiles = rows_in.shape[0], protos // LANES
    sums = rows_in[0]
    for q in range(1, tall):
        sums = sums + rows_in[q]
    inverse_sums = 1.0 / sums[:, :rows]
    for i in range(rows // LANES):
        scale[i // 2, i % 2:i % 2 + 1] = inverse_sums[:, tile(i)]
    if finish:
        piece = rows // tall
        for i in range(rows // LANES):
            each = LANES // piece
            line = [rows_in[each * i + t][:, rows:rows + piece] for t in range(each)]
            extra[i // 2, i % 2:i % 2 + 1] = 10.0 / jnp.concatenate(line, axis=1)
    else:
        extra[...] = sums[:, rows:]

    cols = [jnp.zeros((8, LANES), F32)] * tiles
    for i in range(rows // BLOCK):
        weight = down(scale[i])
        for j in range(tiles):
            value = like[i * BLOCK:(i + 1) * BLOCK, tile(j)]
            cols[j] = cols[j] + fold(value * value * weight)
    result = jnp.concatenate([jnp.sum(c, axis=0, keepdims=True) for c in cols], axis=0)
    if len(col_out.shape) == 3:
        copies(col_out, result)
    else:
        col_out[...] = result


def gradient_kernel(ratio, like, upper, lower, cols_in, rows_in, like_scale, feat_t_a, feat_t_b, unit_proto, basis_t,
                    row_grad, part_t, factor_mine, factor_other, code_scale, gradient, grads, sent):
    factor = 1.0 / add4(*(cols_in[i] for i in range(4)))
    code_scale[...] = (10.0 / jnp.sum(rows_in[...], axis=0)).reshape(code_scale.shape)
    mine = factor_mine.shape[0]
    basis = basis_t[...].astype(BF16)
    rows, protos = like.shape
    blocks = rows // BLOCK

    def copy(i):
        here = slice(i * BLOCK, (i + 1) * BLOCK)
        return pltpu.make_async_copy(grads.at[here], row_grad.at[here], sent.at[i])

    for i in range(blocks):
        here = slice(i * BLOCK, (i + 1) * BLOCK)
        table = upper if i < blocks // 2 else lower
        there = slice((i % (blocks // 2)) * BLOCK, (i % (blocks // 2) + 1) * BLOCK)
        first = down(like_scale[i])
        second = down(code_scale[i])
        for j in range(protos // LANES):
            value = like[here, tile(j)] * first - table[there, tile(j)] * factor[j:j + 1, :] * second
            gradient[here, tile(j)] = value.astype(BF16)
        grads[here, :] = dot16(gradient[here, :], unit_proto[...], nn)
        copy(i).start()
    for n in range(protos // BLOCK):
        here = slice(n * BLOCK, (n + 1) * BLOCK)
        part = dot16(feat_t_a[...], gradient[:rows // 2, here], nn)
        part = ratio * (part + dot16(feat_t_b[...], gradient[rows // 2:, here], nn))
        part_t[:, here] = part
        high, low = split(part)
        both = dot16(basis, high, nn) + dot16(basis, low, nn)
        factor_mine[:, here] = both[:mine]
        factor_other[:, here] = both[mine:]
    for i in range(blocks):
        copy(i).wait()


def mixed_kernel(a, b, c, d, part_t, part_other, factor_t, mixed_t):
    total = (a[...] + b[...]) + (c[...] + d[...])
    factor_t[...] = total
    rank = total.shape[0]
    part_high, part_low = split(part_t[...] + part_other[...])
    high, low = split(total)
    both = dot16(jnp.concatenate([high, low], axis=0), part_high, nt)
    mixed_t[...] = both[:rank] + both[rank:] + dot16(high, part_low, nt)


def inverse(gram):
    rank = gram.shape[0]
    row = lax.broadcasted_iota(jnp.int32, (rank, 1), 0)
    unit = (row == lax.broadcasted_iota(jnp.int32, (rank, rank), 1)).astype(F32)
    wide = jnp.concatenate([unit, gram, jnp.zeros((rank, LANES - 2 * rank), F32)], axis=1)
    for j in range(0, rank, PIVOTS):
        lines = [wide[j + t:j + t + 1, :] for t in range(PIVOTS)]
        at = [rank + j + t for t in range(PIVOTS)]
        small = [[jnp.broadcast_to(line[:, k:k + 1], (1, LANES)) for k in at] for line in lines]
        columns = [jnp.broadcast_to(wide[:, k:k + 1], (rank, LANES)) for k in at]
        for t in range(PIVOTS):
            scale = 1.0 / small[t][t]
            lines[t] = lines[t] * scale
            small[t] = [v * scale for v in small[t]]
            for u in range(PIVOTS):
                if u != t:
                    by = small[u][t]
                    lines[u] = lines[u] - by * lines[t]
                    small[u] = [v - by * w for v, w in zip(small[u], small[t])]
        reduced = wide
        for t in range(PIVOTS):
            reduced = reduced - columns[t] * lines[t]
        for t in range(PIVOTS):
            reduced = jnp.where(row == j + t, lines[t], reduced)
        wide = reduced
    return wide[:, :rank]


def final_kernel(mixed_a, mixed_b, mixed_c, mixed_d, basis_t, factor_mine, factor_other, proto_grad):
    mixed = (mixed_a[...] + mixed_b[...]) + (mixed_c[...] + mixed_d[...])
    weights = dot32(inverse(dot32(basis_t[...], mixed, nt)), mixed, nn)
    high, low = split(jnp.concatenate([factor_mine[...], factor_other[...]], axis=0))
    weights_high, weights_low = split(weights)
    proto_grad[...] = dot16(
        jnp.concatenate([high, low, high], axis=0),
        jnp.concatenate([weights_high, weights_high, weights_low], axis=0),
        tn,
    )


def gather_kernel(grads, after, out):
    out[...] = jnp.sum(grads[...], axis=0)


def shape(*dims, dtype=F32):
    return jax.ShapeDtypeStruct(dims, dtype)


def kept(*dims, dtype=F32):
    return pltpu.VMEM(dims, dtype)


def stay(value):
    return pltpu.with_memory_space_constraint(value, pltpu.VMEM)


def call(body, outs, scratch=(), limit=24, flops=0, name=None, ins=None, out_specs=None):
    specs = {}
    if ins is not None:
        specs["in_specs"] = [pl.BlockSpec(memory_space=m) for m in ins]
    if out_specs is not None:
        specs["out_specs"] = tuple(pl.BlockSpec(memory_space=m) for m in out_specs)
    return pl.pallas_call(
        body,
        out_shape=outs,
        scratch_shapes=scratch,
        name=name,
        compiler_params=pltpu.CompilerParams(vmem_limit_bytes=limit * MIB),
        cost_estimate=pl.CostEstimate(flops=flops, bytes_accessed=0, transcendentals=0),
        **specs,
    )


def exchange(value, axes):
    return lax.all_to_all(value, axes, 0, 0)


def sum_core(value):
    return value + lax.ppermute(value, "c", [(0, 1), (1, 0)])


def add4(a, b, c, d):
    return (a + b) + (c + d)


def swap(value, axis, mask):
    return lax.ppermute(value, axis, [(i, i ^ mask) for i in range(lax.axis_size(axis))])


def fours(value, axis):
    return (value,) + tuple(swap(value, axis, m) for m in (1, 3, 2))


def on_device(features, prototypes, sibling_view, q_seed):
    proto = ("y", "z")
    rows, feat = features.shape
    protos = prototypes.shape[0]
    rank = q_seed.shape[1]
    half = rows // 2
    row_tiles, col_tiles, blocks = rows // LANES, protos // LANES, rows // BLOCK
    wide, tall = lax.axis_size(("x", "c")), lax.axis_size(proto)
    deep = lax.axis_size("z")
    ratio = (protos * tall) / (rows * wide)
    per_block = (blocks, BLOCK // LANES, LANES)
    row_scratch = (pltpu.VMEM(per_block, F32),)
    V, H, A = pltpu.VMEM, pltpu.HBM, pl.ANY

    unit_feat, unit_proto, like, cols, total, sibling, seed_t = call(
        scores_kernel,
        (
            shape(rows, feat, dtype=BF16),
            shape(protos, feat, dtype=BF16),
            kept(rows, protos),
            shape(col_tiles, LANES),
            shape(*per_block),
            shape(row_tiles, LANES, dtype=jnp.int32),
            shape(rank, feat, dtype=jnp.int32),
        ),
        (V((rows, feat), BF16), V((protos, feat), BF16), pltpu.SemaphoreType.DMA((4,))),
        name="scores", ins=(H, H, H, H),
    )(
        pltpu.with_memory_space_constraint(features, H),
        pltpu.with_memory_space_constraint(prototypes, H),
        pltpu.with_memory_space_constraint(sibling_view.reshape(row_tiles, LANES), H),
        pltpu.with_memory_space_constraint(q_seed.T, H),
    )

    def sibling_half(first, after, *extra):
        return call(
            functools.partial(sibling_kernel, first),
            (kept(half, protos), shape(feat, half, dtype=BF16)) + extra,
            name="sibling", ins=(V, V, V, V, A), flops=4 * half * rows * feat,
        )(unit_feat, unit_proto, sibling, seed_t, after)

    def row_step(cols, rest, later):
        return call(row_kernel, shape(tall, 1, rows + LANES), name="rows", ins=(V, V, V, A))(
            cols, stay(like), rest, stay(later)
        )

    def column_step(finish, sums, *outs):
        return call(functools.partial(column_kernel, finish), outs, row_scratch, name="columns")(
            sums, stay(like)
        )

    cols = sum_core(cols)
    upper, feat_t_a, basis_t = sibling_half(0, cols, shape(rank, feat))
    cols = jnp.stack(fours(cols, "x"))
    row_sums = exchange(row_step(cols, total, upper), proto)
    cols, piece = column_step(False, row_sums, shape(col_tiles, LANES), shape(1, LANES))
    cols = sum_core(cols)
    lower, feat_t_b = sibling_half(half, cols)
    cols = jnp.stack(fours(cols, "x"))
    row_sums = exchange(row_step(cols, piece, lower), proto)
    cols, like_scale = column_step(True, row_sums, shape(col_tiles, LANES), shape(*per_block))
    cols = jnp.stack(fours(sum_core(cols), "x"))
    row_sums = exchange(
        call(last_row_kernel, shape(tall, row_tiles, LANES), row_scratch, name="rows", ins=(V, V, V, A))(
            cols, stay(upper), stay(lower), stay(like)
        ),
        proto,
    )

    mine = rank // 2
    row_grad, part_t, factor_mine, factor_other = call(
        functools.partial(gradient_kernel, ratio),
        (
            pltpu.HBM((rows, feat), F32),
            shape(feat, protos),
            shape(mine, protos),
            shape(mine, protos),
        ),
        row_scratch
        + (V((rows, protos), BF16), V((rows, feat), F32), pltpu.SemaphoreType.DMA((blocks,))),
        name="gradient", ins=(V,) * 10, out_specs=(H, V, V, V),
    )(
        stay(like), stay(upper), stay(lower), cols, row_sums, like_scale, feat_t_a, feat_t_b, unit_proto,
        basis_t,
    )
    factor_mine, part_t = lax.optimization_barrier((factor_mine + swap(factor_other, "c", 1), part_t))
    grads = exchange(row_grad.reshape(tall // deep, -1, feat), "y")

    factor_mine, mixed_t = call(
        mixed_kernel, (shape(mine, protos), shape(mine, feat)), name="mixed",
    )(*fours(factor_mine, "x"), part_t, swap(part_t, "c", 1))
    factor_other = swap(factor_mine, "c", 1)
    mixed_t = add4(*fours(mixed_t, "z"))
    mixed_t = mixed_t + swap(mixed_t, "z", 4)
    mixed_other = swap(mixed_t, "c", 1)
    grads = call(gather_kernel, shape(deep * rows // tall, feat), name="gather", ins=(V, A))(
        grads, mixed_other
    )
    mixed_t = jnp.concatenate([mixed_t, mixed_other], axis=0)
    grads = exchange(grads.reshape(deep, rows // tall, feat), "z")
    mixed_t = add4(*fours(mixed_t, "x"))
    proto_grad = call(final_kernel, shape(protos, feat), name="final")(
        *fours(mixed_t, "y"), basis_t, factor_mine, factor_other
    )
    return jnp.sum(grads, axis=0), proto_grad


def solution(mesh):
    wide, tall = mesh.shape["dp"], mesh.shape["proto"]
    fine = Mesh(mesh.devices.reshape(wide // 2, 2, 4, tall // 4), ("x", "c", "y", "z"))
    dp, proto = ("x", "c"), ("y", "z")
    return jax.shard_map(
        on_device,
        mesh=fine,
        in_specs=(P(dp, None), P(proto, None), P(dp), P()),
        out_specs=(P(dp + proto, None), P(proto, None)),
        check_vma=False,
    )
```

```python
import functools
import math

import jax
import jax.numpy as jnp
from jax import lax
from jax.experimental import pallas as pl
from jax.experimental.pallas import tpu as pltpu
from jax.sharding import Mesh, PartitionSpec as P

epsilon = 1e-06
highest = lax.Precision.HIGHEST
F32, BF16 = jnp.float32, jnp.bfloat16
LANES = 128
BLOCK = 256
PIVOTS = 8
MIB = 1 << 20

nt = (((1,), (1,)), ((), ()))
nn = (((1,), (0,)), ((), ()))
tn = (((0,), (0,)), ((), ()))


def dot32(a, b, dims):
    return lax.dot_general(a, b, dims, precision=highest, preferred_element_type=F32)


def dot16(a, b, dims):
    return lax.dot_general(a, b, dims, preferred_element_type=F32)


def split(value):
    high = value.astype(BF16)
    return high, (value - high.astype(F32)).astype(BF16)


def unit_rows(block):
    wide = block.astype(F32)
    return (wide * lax.rsqrt(jnp.sum(wide * wide, axis=-1, keepdims=True) + epsilon)).astype(BF16)


def across(partial):
    count = partial.shape[0] // LANES
    return jnp.concatenate(
        [jnp.sum(partial[i * LANES:(i + 1) * LANES].T, axis=0, keepdims=True) for i in range(count)],
        axis=0,
    )


def down(rows):
    return jnp.concatenate(
        [jnp.broadcast_to(rows[i:i + 1], (LANES, LANES)).T for i in range(rows.shape[0])], axis=0
    )


def tile(j):
    return slice(j * LANES, (j + 1) * LANES)


def fold(value):
    return jnp.sum(value.reshape(-1, 8, LANES), axis=0)


def copies(ref, value):
    for i in range(ref.shape[0]):
        ref[i] = value


def scores_kernel(feat_hbm, proto_hbm, sibling_hbm, seed_hbm, unit_feat, unit_proto, like, col_out, total,
                  sibling, seed_t, feat, proto, ready):
    rows, protos = feat.shape[0], proto.shape[0]
    tiles = protos // LANES
    proto_copy = pltpu.make_async_copy(proto_hbm, proto, ready.at[0])
    feat_copy = pltpu.make_async_copy(feat_hbm, feat, ready.at[1])
    sibling_copy = pltpu.make_async_copy(sibling_hbm, sibling, ready.at[2])
    seed_copy = pltpu.make_async_copy(seed_hbm, seed_t, ready.at[3])
    proto_copy.start()
    feat_copy.start()
    sibling_copy.start()
    seed_copy.start()
    proto_copy.wait()
    unit_proto[...] = unit_rows(proto[...])
    feat_copy.wait()

    cols = [jnp.zeros((8, LANES), F32)] * tiles
    for i in range(rows // BLOCK):
        here = slice(i * BLOCK, (i + 1) * BLOCK)
        unit = unit_rows(feat[here, :])
        unit_feat[here, :] = unit
        value = jnp.exp(dot16(unit, unit_proto[...], nt) * 10.0)
        like[here, :] = value
        part = value[:, tile(0)]
        for j in range(1, tiles):
            part = part + value[:, tile(j)]
        total[i] = across(part)
        square = value * value
        cols = [cols[j] + fold(square[:, tile(j)]) for j in range(tiles)]
    col_out[...] = jnp.concatenate([jnp.sum(c, axis=0, keepdims=True) for c in cols], axis=0)
    sibling_copy.wait()
    seed_copy.wait()


def sibling_kernel(first, unit_feat, unit_proto, sibling, seed_t, after, energy, unit_feat_t, *basis_t):
    rows = unit_feat.shape[0]
    for out in basis_t:
        seed = seed_t[...].astype(F32) * 0.125
        mine = seed.shape[0] // 2
        turned = jnp.concatenate([seed[mine:], seed[:mine]], axis=0)
        out[...] = jnp.where(lax.axis_index("c") == 0, seed, turned)

    for i in range(energy.shape[0] // BLOCK):
        here = slice(i * BLOCK, (i + 1) * BLOCK)
        there = slice(first + i * BLOCK, first + (i + 1) * BLOCK)
        row = lax.broadcasted_iota(jnp.int32, (BLOCK, LANES), 0) + (first + i * BLOCK)
        pick = [
            jnp.where(row == sibling[j:j + 1, :], 1.0, 0.0).astype(BF16) for j in range(rows // LANES)
        ]
        feats = dot16(jnp.concatenate(pick, axis=1), unit_feat[...], nn).astype(BF16)
        energy[here, :] = jnp.exp(dot16(feats, unit_proto[...], nt) * 20.0)
        unit_feat_t[:, here] = unit_feat[there, :].T


def flat(rows):
    return jnp.concatenate([rows[i:i + 1] for i in range(rows.shape[0])], axis=1)


def row_kernel(a, b, c, d, like, rest, later, row_out):
    factor = 1.0 / add4(a[...], b[...], c[...], d[...])
    rows, protos = like.shape
    sums = []
    for i in range(rows // BLOCK):
        part = None
        for j in range(protos // LANES):
            value = like[i * BLOCK:(i + 1) * BLOCK, tile(j)]
            value = value * value * factor[j:j + 1, :]
            part = value if part is None else part + value
        sums.append(flat(across(part)))
    result = jnp.concatenate(sums, axis=1)
    tall = row_out.shape[0]
    piece = rows // tall
    if rest.shape[0] == 1:
        tails = [rest[...]] * tall
    else:
        totals = rest[...].reshape(rows // LANES, LANES)
        tails = [
            totals[q * piece // LANES:q * piece // LANES + 1, q * piece % LANES:q * piece % LANES + piece]
            for q in range(tall)
        ]
        tails = [jnp.concatenate([t, jnp.zeros((1, LANES - piece), F32)], axis=1) for t in tails]
    for q in range(tall):
        row_out[q] = jnp.concatenate([result, tails[q]], axis=1)


def last_row_kernel(a, b, c, d, upper, lower, like, row_out, factor_out, sums):
    factor = 1.0 / add4(a[...], b[...], c[...], d[...])
    factor_out[...] = factor
    half, protos = upper.shape
    for number, table in enumerate((upper, lower)):
        for i in range(half // BLOCK):
            part = None
            for j in range(protos // LANES):
                value = table[i * BLOCK:(i + 1) * BLOCK, tile(j)] * factor[j:j + 1, :]
                part = value if part is None else part + value
            sums[number * (half // BLOCK) + i] = across(part)
    copies(row_out, sums[...].reshape(row_out.shape[1:]))


def column_kernel(finish, rows_in, like, col_out, extra, scale):
    rows, protos = like.shape
    tall, tiles = rows_in.shape[0], protos // LANES
    sums = rows_in[0]
    for q in range(1, tall):
        sums = sums + rows_in[q]
    inverse_sums = 1.0 / sums[:, :rows]
    for i in range(rows // LANES):
        scale[i // 2, i % 2:i % 2 + 1] = inverse_sums[:, tile(i)]
    if finish:
        piece = rows // tall
        for i in range(rows // LANES):
            each = LANES // piece
            line = [rows_in[each * i + t][:, rows:rows + piece] for t in range(each)]
            extra[i // 2, i % 2:i % 2 + 1] = 10.0 / jnp.concatenate(line, axis=1)
    else:
        extra[...] = sums[:, rows:]

    cols = [jnp.zeros((8, LANES), F32)] * tiles
    for i in range(rows // BLOCK):
        weight = down(scale[i])
        for j in range(tiles):
            value = like[i * BLOCK:(i + 1) * BLOCK, tile(j)]
            cols[j] = cols[j] + fold(value * value * weight)
    result = jnp.concatenate([jnp.sum(c, axis=0, keepdims=True) for c in cols], axis=0)
    if len(col_out.shape) == 3:
        copies(col_out, result)
    else:
        col_out[...] = result


def gradient_kernel(ratio, like, upper, lower, factor, rows_in, like_scale, feat_t_a, feat_t_b, unit_proto, basis_t,
                    row_grad, part_t, factor_mine, factor_other, code_scale, gradient, grads, sent):
    code_scale[...] = (10.0 / jnp.sum(rows_in[...], axis=0)).reshape(code_scale.shape)
    mine = factor_mine.shape[0]
    basis = basis_t[...].astype(BF16)
    rows, protos = like.shape
    blocks = rows // BLOCK

    def copy(i):
        here = slice(i * BLOCK, (i + 1) * BLOCK)
        return pltpu.make_async_copy(grads.at[here], row_grad.at[here], sent.at[i])

    for i in range(blocks):
        here = slice(i * BLOCK, (i + 1) * BLOCK)
        table = upper if i < blocks // 2 else lower
        there = slice((i % (blocks // 2)) * BLOCK, (i % (blocks // 2) + 1) * BLOCK)
        first = down(like_scale[i])
        second = down(code_scale[i])
        for j in range(protos // LANES):
            value = like[here, tile(j)] * first - table[there, tile(j)] * factor[j:j + 1, :] * second
            gradient[here, tile(j)] = value.astype(BF16)
        grads[here, :] = dot16(gradient[here, :], unit_proto[...], nn)
        copy(i).start()
    for n in range(protos // BLOCK):
        here = slice(n * BLOCK, (n + 1) * BLOCK)
        part = dot16(feat_t_a[...], gradient[:rows // 2, here], nn)
        part = ratio * (part + dot16(feat_t_b[...], gradient[rows // 2:, here], nn))
        part_t[:, here] = part
        high, low = split(part)
        both = dot16(basis, high, nn) + dot16(basis, low, nn)
        factor_mine[:, here] = both[:mine]
        factor_other[:, here] = both[mine:]
    for i in range(blocks):
        copy(i).wait()


def mixed_kernel(a, b, c, d, part_t, part_other, factor_t, mixed_t):
    total = (a[...] + b[...]) + (c[...] + d[...])
    factor_t[...] = total
    rank = total.shape[0]
    part_high, part_low = split(part_t[...] + part_other[...])
    high, low = split(total)
    both = dot16(jnp.concatenate([high, low], axis=0), part_high, nt)
    mixed_t[...] = both[:rank] + both[rank:] + dot16(high, part_low, nt)


def inverse(gram):
    rank = gram.shape[0]
    row = lax.broadcasted_iota(jnp.int32, (rank, 1), 0)
    unit = (row == lax.broadcasted_iota(jnp.int32, (rank, rank), 1)).astype(F32)
    wide = jnp.concatenate([unit, gram, jnp.zeros((rank, LANES - 2 * rank), F32)], axis=1)
    for j in range(0, rank, PIVOTS):
        lines = [wide[j + t:j + t + 1, :] for t in range(PIVOTS)]
        at = [rank + j + t for t in range(PIVOTS)]
        small = [[jnp.broadcast_to(line[:, k:k + 1], (1, LANES)) for k in at] for line in lines]
        columns = [jnp.broadcast_to(wide[:, k:k + 1], (rank, LANES)) for k in at]
        for t in range(PIVOTS):
            scale = 1.0 / small[t][t]
            lines[t] = lines[t] * scale
            small[t] = [v * scale for v in small[t]]
            for u in range(PIVOTS):
                if u != t:
                    by = small[u][t]
                    lines[u] = lines[u] - by * lines[t]
                    small[u] = [v - by * w for v, w in zip(small[u], small[t])]
        reduced = wide
        for t in range(PIVOTS):
            reduced = reduced - columns[t] * lines[t]
        for t in range(PIVOTS):
            reduced = jnp.where(row == j + t, lines[t], reduced)
        wide = reduced
    return wide[:, :rank]


def final_kernel(mixed_a, mixed_b, mixed_c, mixed_d, basis_t, factor_mine, factor_other, proto_grad):
    mixed = (mixed_a[...] + mixed_b[...]) + (mixed_c[...] + mixed_d[...])
    weights = dot32(inverse(dot32(basis_t[...], mixed, nt)), mixed, nn)
    high, low = split(jnp.concatenate([factor_mine[...], factor_other[...]], axis=0))
    weights_high, weights_low = split(weights)
    proto_grad[...] = dot16(
        jnp.concatenate([high, low, high], axis=0),
        jnp.concatenate([weights_high, weights_high, weights_low], axis=0),
        tn,
    )


def gather_kernel(grads, after, out):
    out[...] = jnp.sum(grads[...], axis=0)


def shape(*dims, dtype=F32):
    return jax.ShapeDtypeStruct(dims, dtype)


def kept(*dims, dtype=F32):
    return pltpu.VMEM(dims, dtype)


def stay(value):
    return pltpu.with_memory_space_constraint(value, pltpu.VMEM)


def call(body, outs, scratch=(), limit=24, flops=0, name=None, ins=None, out_specs=None):
    specs = {}
    if ins is not None:
        specs["in_specs"] = [pl.BlockSpec(memory_space=m) for m in ins]
    if out_specs is not None:
        specs["out_specs"] = tuple(pl.BlockSpec(memory_space=m) for m in out_specs)
    return pl.pallas_call(
        body,
        out_shape=outs,
        scratch_shapes=scratch,
        name=name,
        compiler_params=pltpu.CompilerParams(vmem_limit_bytes=limit * MIB),
        cost_estimate=pl.CostEstimate(flops=flops, bytes_accessed=0, transcendentals=0),
        **specs,
    )


def exchange(value, axes):
    return lax.all_to_all(value, axes, 0, 0)


def sum_core(value):
    return value + lax.ppermute(value, "c", [(0, 1), (1, 0)])


def add4(a, b, c, d):
    return (a + b) + (c + d)


def swap(value, axis, mask):
    return lax.ppermute(value, axis, [(i, i ^ mask) for i in range(lax.axis_size(axis))])


def fours(value, axis):
    return (value,) + tuple(swap(value, axis, m) for m in (1, 3, 2))


def on_device(features, prototypes, sibling_view, q_seed):
    proto = ("y", "z")
    rows, feat = features.shape
    protos = prototypes.shape[0]
    rank = q_seed.shape[1]
    half = rows // 2
    row_tiles, col_tiles, blocks = rows // LANES, protos // LANES, rows // BLOCK
    wide, tall = lax.axis_size(("x", "c")), lax.axis_size(proto)
    deep = lax.axis_size("z")
    ratio = (protos * tall) / (rows * wide)
    per_block = (blocks, BLOCK // LANES, LANES)
    row_scratch = (pltpu.VMEM(per_block, F32),)
    V, H, A = pltpu.VMEM, pltpu.HBM, pl.ANY

    unit_feat, unit_proto, like, cols, total, sibling, seed_t = call(
        scores_kernel,
        (
            shape(rows, feat, dtype=BF16),
            shape(protos, feat, dtype=BF16),
            kept(rows, protos),
            shape(col_tiles, LANES),
            shape(*per_block),
            shape(row_tiles, LANES, dtype=jnp.int32),
            shape(rank, feat, dtype=jnp.int32),
        ),
        (V((rows, feat), BF16), V((protos, feat), BF16), pltpu.SemaphoreType.DMA((4,))),
        name="scores", ins=(H, H, H, H),
    )(
        pltpu.with_memory_space_constraint(features, H),
        pltpu.with_memory_space_constraint(prototypes, H),
        pltpu.with_memory_space_constraint(sibling_view.reshape(row_tiles, LANES), H),
        pltpu.with_memory_space_constraint(q_seed.T, H),
    )

    def sibling_half(first, after, *extra):
        return call(
            functools.partial(sibling_kernel, first),
            (kept(half, protos), shape(feat, half, dtype=BF16)) + extra,
            name="sibling", ins=(V, V, V, V, A), flops=4 * half * rows * feat,
        )(unit_feat, unit_proto, sibling, seed_t, after)

    def row_step(cols, rest, later):
        return call(row_kernel, shape(tall, 1, rows + LANES), name="rows", ins=(V,) * 6 + (A,))(
            *cols, stay(like), rest, stay(later)
        )

    def column_step(finish, sums, *outs):
        return call(functools.partial(column_kernel, finish), outs, row_scratch, name="columns")(
            sums, stay(like)
        )

    cols = sum_core(cols)
    upper, feat_t_a, basis_t = sibling_half(0, cols, shape(rank, feat))
    cols = fours(cols, "x")
    row_sums = exchange(row_step(cols, total, upper), proto)
    cols, piece = column_step(False, row_sums, shape(col_tiles, LANES), shape(1, LANES))
    cols = sum_core(cols)
    lower, feat_t_b = sibling_half(half, cols)
    cols = fours(cols, "x")
    row_sums = exchange(row_step(cols, piece, lower), proto)
    cols, like_scale = column_step(True, row_sums, shape(col_tiles, LANES), shape(*per_block))
    cols = fours(sum_core(cols), "x")
    row_sums, factor = call(
        last_row_kernel, (shape(tall, row_tiles, LANES), shape(col_tiles, LANES)), row_scratch,
        name="rows", ins=(V,) * 6 + (A,),
    )(*cols, stay(upper), stay(lower), stay(like))
    row_sums = exchange(row_sums, proto)

    mine = rank // 2
    row_grad, part_t, factor_mine, factor_other = call(
        functools.partial(gradient_kernel, ratio),
        (
            pltpu.HBM((rows, feat), F32),
            shape(feat, protos),
            shape(mine, protos),
            shape(mine, protos),
        ),
        row_scratch
        + (V((rows, protos), BF16), V((rows, feat), F32), pltpu.SemaphoreType.DMA((blocks,))),
        name="gradient", ins=(V,) * 10, out_specs=(H, V, V, V),
    )(
        stay(like), stay(upper), stay(lower), factor, row_sums, like_scale, feat_t_a, feat_t_b, unit_proto,
        basis_t,
    )
    factor_mine, part_t = lax.optimization_barrier((factor_mine + swap(factor_other, "c", 1), part_t))
    grads = exchange(row_grad.reshape(tall // deep, -1, feat), "y")

    factor_mine, mixed_t = call(
        mixed_kernel, (shape(mine, protos), shape(mine, feat)), name="mixed",
    )(*fours(factor_mine, "x"), part_t, swap(part_t, "c", 1))
    factor_other = swap(factor_mine, "c", 1)
    mixed_t = mixed_t + swap(mixed_t, "z", 1)
    mixed_t = add4(mixed_t, *(swap(mixed_t, "z", m) for m in (2, 6, 4)))
    mixed_other = swap(mixed_t, "c", 1)
    grads = call(gather_kernel, shape(deep * rows // tall, feat), name="gather", ins=(V, A))(
        grads, mixed_other
    )
    mixed_t = jnp.concatenate([mixed_t, mixed_other], axis=0)
    grads = exchange(grads.reshape(deep, rows // tall, feat), "z")
    mixed_t = add4(*fours(mixed_t, "x"))
    proto_grad = call(final_kernel, shape(protos, feat), name="final")(
        *fours(mixed_t, "y"), basis_t, factor_mine, factor_other
    )
    return jnp.sum(grads, axis=0), proto_grad


def solution(mesh):
    wide, tall = mesh.shape["dp"], mesh.shape["proto"]
    fine = Mesh(mesh.devices.reshape(wide // 2, 2, 4, tall // 4), ("x", "c", "y", "z"))
    dp, proto = ("x", "c"), ("y", "z")
    return jax.shard_map(
        on_device,
        mesh=fine,
        in_specs=(P(dp, None), P(proto, None), P(dp), P()),
        out_specs=(P(dp + proto, None), P(proto, None)),
        check_vma=False,
    )
```

```python
import functools
import math

import jax
import jax.numpy as jnp
from jax import lax
from jax.experimental import pallas as pl
from jax.experimental.pallas import tpu as pltpu
from jax.sharding import Mesh, PartitionSpec as P

epsilon = 1e-06
highest = lax.Precision.HIGHEST
F32, BF16 = jnp.float32, jnp.bfloat16
LANES = 128
BLOCK = 256
PIVOTS = 8
MIB = 1 << 20

nt = (((1,), (1,)), ((), ()))
nn = (((1,), (0,)), ((), ()))
tn = (((0,), (0,)), ((), ()))


def dot32(a, b, dims):
    return lax.dot_general(a, b, dims, precision=highest, preferred_element_type=F32)


def dot16(a, b, dims):
    return lax.dot_general(a, b, dims, preferred_element_type=F32)


def split(value):
    high = value.astype(BF16)
    return high, (value - high.astype(F32)).astype(BF16)


def unit_rows(block):
    wide = block.astype(F32)
    return (wide * lax.rsqrt(jnp.sum(wide * wide, axis=-1, keepdims=True) + epsilon)).astype(BF16)


def across(partial):
    count = partial.shape[0] // LANES
    return jnp.concatenate(
        [jnp.sum(partial[i * LANES:(i + 1) * LANES].T, axis=0, keepdims=True) for i in range(count)],
        axis=0,
    )


def down(rows):
    return jnp.concatenate(
        [jnp.broadcast_to(rows[i:i + 1], (LANES, LANES)).T for i in range(rows.shape[0])], axis=0
    )


def tile(j):
    return slice(j * LANES, (j + 1) * LANES)


def fold(value):
    return jnp.sum(value.reshape(-1, 8, LANES), axis=0)


def copies(ref, value):
    for i in range(ref.shape[0]):
        ref[i] = value


def scores_kernel(feat_hbm, proto_hbm, sibling_hbm, seed_hbm, unit_feat, unit_proto, like, col_out, total,
                  sibling, seed_t, feat, proto, ready):
    rows, protos = feat.shape[0], proto.shape[0]
    tiles = protos // LANES
    proto_copy = pltpu.make_async_copy(proto_hbm, proto, ready.at[0])
    feat_copy = pltpu.make_async_copy(feat_hbm, feat, ready.at[1])
    sibling_copy = pltpu.make_async_copy(sibling_hbm, sibling, ready.at[2])
    seed_copy = pltpu.make_async_copy(seed_hbm, seed_t, ready.at[3])
    proto_copy.start()
    feat_copy.start()
    sibling_copy.start()
    seed_copy.start()
    proto_copy.wait()
    unit_proto[...] = unit_rows(proto[...])
    feat_copy.wait()

    cols = [jnp.zeros((8, LANES), F32)] * tiles
    for i in range(rows // BLOCK):
        here = slice(i * BLOCK, (i + 1) * BLOCK)
        unit = unit_rows(feat[here, :])
        unit_feat[here, :] = unit
        value = jnp.exp(dot16(unit, unit_proto[...], nt) * 10.0)
        part = value[:, tile(0)]
        for j in range(1, tiles):
            part = part + value[:, tile(j)]
        total[i] = across(part)
        square = value * value
        like[here, :] = square
        cols = [cols[j] + fold(square[:, tile(j)]) for j in range(tiles)]
    col_out[...] = jnp.concatenate([jnp.sum(c, axis=0, keepdims=True) for c in cols], axis=0)
    sibling_copy.wait()
    seed_copy.wait()


def sibling_kernel(first, unit_feat, unit_proto, sibling, seed_t, after, energy, unit_feat_t, *basis_t):
    rows = unit_feat.shape[0]
    for out in basis_t:
        seed = seed_t[...].astype(F32) * 0.125
        mine = seed.shape[0] // 2
        turned = jnp.concatenate([seed[mine:], seed[:mine]], axis=0)
        out[...] = jnp.where(lax.axis_index("c") == 0, seed, turned)

    for i in range(energy.shape[0] // BLOCK):
        here = slice(i * BLOCK, (i + 1) * BLOCK)
        there = slice(first + i * BLOCK, first + (i + 1) * BLOCK)
        row = lax.broadcasted_iota(jnp.int32, (BLOCK, LANES), 0) + (first + i * BLOCK)
        pick = [
            jnp.where(row == sibling[j:j + 1, :], 1.0, 0.0).astype(BF16) for j in range(rows // LANES)
        ]
        feats = dot16(jnp.concatenate(pick, axis=1), unit_feat[...], nn).astype(BF16)
        energy[here, :] = jnp.exp(dot16(feats, unit_proto[...], nt) * 20.0)
        unit_feat_t[:, here] = unit_feat[there, :].T


def flat(rows):
    return jnp.concatenate([rows[i:i + 1] for i in range(rows.shape[0])], axis=1)


def row_kernel(a, b, c, d, like, rest, later, row_out):
    factor = 1.0 / add4(a[...], b[...], c[...], d[...])
    rows, protos = like.shape
    sums = []
    for i in range(rows // BLOCK):
        part = None
        for j in range(protos // LANES):
            value = like[i * BLOCK:(i + 1) * BLOCK, tile(j)]
            value = value * factor[j:j + 1, :]
            part = value if part is None else part + value
        sums.append(flat(across(part)))
    result = jnp.concatenate(sums, axis=1)
    tall = row_out.shape[0]
    piece = rows // tall
    if rest.shape[0] == 1:
        tails = [rest[...]] * tall
    else:
        totals = rest[...].reshape(rows // LANES, LANES)
        tails = [
            totals[q * piece // LANES:q * piece // LANES + 1, q * piece % LANES:q * piece % LANES + piece]
            for q in range(tall)
        ]
        tails = [jnp.concatenate([t, jnp.zeros((1, LANES - piece), F32)], axis=1) for t in tails]
    for q in range(tall):
        row_out[q] = jnp.concatenate([result, tails[q]], axis=1)


def last_row_kernel(a, b, c, d, upper, lower, like, row_out, factor_out, sums):
    factor = 1.0 / add4(a[...], b[...], c[...], d[...])
    factor_out[...] = factor
    half, protos = upper.shape
    for number, table in enumerate((upper, lower)):
        for i in range(half // BLOCK):
            part = None
            for j in range(protos // LANES):
                value = table[i * BLOCK:(i + 1) * BLOCK, tile(j)] * factor[j:j + 1, :]
                part = value if part is None else part + value
            sums[number * (half // BLOCK) + i] = across(part)
    copies(row_out, sums[...].reshape(row_out.shape[1:]))


def column_kernel(finish, rows_in, like, col_out, extra, scale):
    rows, protos = like.shape
    tall, tiles = rows_in.shape[0], protos // LANES
    sums = rows_in[0]
    for q in range(1, tall):
        sums = sums + rows_in[q]
    inverse_sums = 1.0 / sums[:, :rows]
    for i in range(rows // LANES):
        scale[i // 2, i % 2:i % 2 + 1] = inverse_sums[:, tile(i)]
    if finish:
        piece = rows // tall
        for i in range(rows // LANES):
            each = LANES // piece
            line = [rows_in[each * i + t][:, rows:rows + piece] for t in range(each)]
            extra[i // 2, i % 2:i % 2 + 1] = 10.0 / jnp.concatenate(line, axis=1)
    else:
        extra[...] = sums[:, rows:]

    cols = [jnp.zeros((8, LANES), F32)] * tiles
    for i in range(rows // BLOCK):
        weight = down(scale[i])
        for j in range(tiles):
            value = like[i * BLOCK:(i + 1) * BLOCK, tile(j)]
            cols[j] = cols[j] + fold(value * weight)
    result = jnp.concatenate([jnp.sum(c, axis=0, keepdims=True) for c in cols], axis=0)
    if len(col_out.shape) == 3:
        copies(col_out, result)
    else:
        col_out[...] = result


def gradient_kernel(ratio, like, upper, lower, factor, rows_in, like_scale, feat_t_a, feat_t_b, unit_proto, basis_t,
                    row_grad, part_t, factor_mine, factor_other, code_scale, gradient, grads, sent):
    code_scale[...] = (10.0 / jnp.sum(rows_in[...], axis=0)).reshape(code_scale.shape)
    mine = factor_mine.shape[0]
    basis = basis_t[...].astype(BF16)
    rows, protos = like.shape
    blocks = rows // BLOCK

    def copy(i):
        here = slice(i * BLOCK, (i + 1) * BLOCK)
        return pltpu.make_async_copy(grads.at[here], row_grad.at[here], sent.at[i])

    for i in range(blocks):
        here = slice(i * BLOCK, (i + 1) * BLOCK)
        table = upper if i < blocks // 2 else lower
        there = slice((i % (blocks // 2)) * BLOCK, (i % (blocks // 2) + 1) * BLOCK)
        first = down(like_scale[i])
        second = down(code_scale[i])
        for j in range(protos // LANES):
            square = like[here, tile(j)]
            value = square * lax.rsqrt(square) * first - table[there, tile(j)] * factor[j:j + 1, :] * second
            gradient[here, tile(j)] = value.astype(BF16)
        grads[here, :] = dot16(gradient[here, :], unit_proto[...], nn)
        copy(i).start()
    for n in range(protos // BLOCK):
        here = slice(n * BLOCK, (n + 1) * BLOCK)
        part = dot16(feat_t_a[...], gradient[:rows // 2, here], nn)
        part = ratio * (part + dot16(feat_t_b[...], gradient[rows // 2:, here], nn))
        part_t[:, here] = part
        high, low = split(part)
        both = dot16(basis, high, nn) + dot16(basis, low, nn)
        factor_mine[:, here] = both[:mine]
        factor_other[:, here] = both[mine:]
    for i in range(blocks):
        copy(i).wait()


def mixed_kernel(a, b, c, d, part_t, part_other, factor_t, mixed_t):
    total = (a[...] + b[...]) + (c[...] + d[...])
    factor_t[...] = total
    rank = total.shape[0]
    part_high, part_low = split(part_t[...] + part_other[...])
    high, low = split(total)
    both = dot16(jnp.concatenate([high, low], axis=0), part_high, nt)
    mixed_t[...] = both[:rank] + both[rank:] + dot16(high, part_low, nt)


def inverse(gram):
    rank = gram.shape[0]
    row = lax.broadcasted_iota(jnp.int32, (rank, 1), 0)
    unit = (row == lax.broadcasted_iota(jnp.int32, (rank, rank), 1)).astype(F32)
    wide = jnp.concatenate([unit, gram, jnp.zeros((rank, LANES - 2 * rank), F32)], axis=1)
    for j in range(0, rank, PIVOTS):
        lines = [wide[j + t:j + t + 1, :] for t in range(PIVOTS)]
        at = [rank + j + t for t in range(PIVOTS)]
        small = [[jnp.broadcast_to(line[:, k:k + 1], (1, LANES)) for k in at] for line in lines]
        columns = [jnp.broadcast_to(wide[:, k:k + 1], (rank, LANES)) for k in at]
        for t in range(PIVOTS):
            scale = 1.0 / small[t][t]
            lines[t] = lines[t] * scale
            small[t] = [v * scale for v in small[t]]
            for u in range(PIVOTS):
                if u != t:
                    by = small[u][t]
                    lines[u] = lines[u] - by * lines[t]
                    small[u] = [v - by * w for v, w in zip(small[u], small[t])]
        reduced = wide
        for t in range(PIVOTS):
            reduced = reduced - columns[t] * lines[t]
        for t in range(PIVOTS):
            reduced = jnp.where(row == j + t, lines[t], reduced)
        wide = reduced
    return wide[:, :rank]


def final_kernel(mixed_a, mixed_b, mixed_c, mixed_d, basis_t, factor_mine, factor_other, proto_grad):
    mixed = (mixed_a[...] + mixed_b[...]) + (mixed_c[...] + mixed_d[...])
    weights = dot32(inverse(dot32(basis_t[...], mixed, nt)), mixed, nn)
    high, low = split(jnp.concatenate([factor_mine[...], factor_other[...]], axis=0))
    weights_high, weights_low = split(weights)
    proto_grad[...] = dot16(
        jnp.concatenate([high, low, high], axis=0),
        jnp.concatenate([weights_high, weights_high, weights_low], axis=0),
        tn,
    )


def gather_kernel(grads, after, out):
    out[...] = jnp.sum(grads[...], axis=0)


def shape(*dims, dtype=F32):
    return jax.ShapeDtypeStruct(dims, dtype)


def kept(*dims, dtype=F32):
    return pltpu.VMEM(dims, dtype)


def stay(value):
    return pltpu.with_memory_space_constraint(value, pltpu.VMEM)


def call(body, outs, scratch=(), limit=24, flops=0, name=None, ins=None, out_specs=None):
    specs = {}
    if ins is not None:
        specs["in_specs"] = [pl.BlockSpec(memory_space=m) for m in ins]
    if out_specs is not None:
        specs["out_specs"] = tuple(pl.BlockSpec(memory_space=m) for m in out_specs)
    return pl.pallas_call(
        body,
        out_shape=outs,
        scratch_shapes=scratch,
        name=name,
        compiler_params=pltpu.CompilerParams(vmem_limit_bytes=limit * MIB),
        cost_estimate=pl.CostEstimate(flops=flops, bytes_accessed=0, transcendentals=0),
        **specs,
    )


def exchange(value, axes):
    return lax.all_to_all(value, axes, 0, 0)


def sum_core(value):
    return value + lax.ppermute(value, "c", [(0, 1), (1, 0)])


def add4(a, b, c, d):
    return (a + b) + (c + d)


def swap(value, axis, mask):
    return lax.ppermute(value, axis, [(i, i ^ mask) for i in range(lax.axis_size(axis))])


def fours(value, axis):
    return (value,) + tuple(swap(value, axis, m) for m in (1, 3, 2))


def on_device(features, prototypes, sibling_view, q_seed):
    proto = ("y", "z")
    rows, feat = features.shape
    protos = prototypes.shape[0]
    rank = q_seed.shape[1]
    half = rows // 2
    row_tiles, col_tiles, blocks = rows // LANES, protos // LANES, rows // BLOCK
    wide, tall = lax.axis_size(("x", "c")), lax.axis_size(proto)
    deep = lax.axis_size("z")
    ratio = (protos * tall) / (rows * wide)
    per_block = (blocks, BLOCK // LANES, LANES)
    row_scratch = (pltpu.VMEM(per_block, F32),)
    V, H, A = pltpu.VMEM, pltpu.HBM, pl.ANY

    unit_feat, unit_proto, like, cols, total, sibling, seed_t = call(
        scores_kernel,
        (
            shape(rows, feat, dtype=BF16),
            shape(protos, feat, dtype=BF16),
            kept(rows, protos),
            shape(col_tiles, LANES),
            shape(*per_block),
            shape(row_tiles, LANES, dtype=jnp.int32),
            shape(rank, feat, dtype=jnp.int32),
        ),
        (V((rows, feat), BF16), V((protos, feat), BF16), pltpu.SemaphoreType.DMA((4,))),
        name="scores", ins=(H, H, H, H),
    )(
        pltpu.with_memory_space_constraint(features, H),
        pltpu.with_memory_space_constraint(prototypes, H),
        pltpu.with_memory_space_constraint(sibling_view.reshape(row_tiles, LANES), H),
        pltpu.with_memory_space_constraint(q_seed.T, H),
    )

    def sibling_half(first, after, *extra):
        return call(
            functools.partial(sibling_kernel, first),
            (kept(half, protos), shape(feat, half, dtype=BF16)) + extra,
            name="sibling", ins=(V, V, V, V, A), flops=4 * half * rows * feat,
        )(unit_feat, unit_proto, sibling, seed_t, after)

    def row_step(cols, rest, later):
        return call(row_kernel, shape(tall, 1, rows + LANES), name="rows", ins=(V,) * 6 + (A,))(
            *cols, stay(like), rest, stay(later)
        )

    def column_step(finish, sums, *outs):
        return call(functools.partial(column_kernel, finish), outs, row_scratch, name="columns")(
            sums, stay(like)
        )

    cols = sum_core(cols)
    upper, feat_t_a, basis_t = sibling_half(0, cols, shape(rank, feat))
    cols = fours(cols, "x")
    row_sums = exchange(row_step(cols, total, upper), proto)
    cols, piece = column_step(False, row_sums, shape(col_tiles, LANES), shape(1, LANES))
    cols = sum_core(cols)
    lower, feat_t_b = sibling_half(half, cols)
    cols = fours(cols, "x")
    row_sums = exchange(row_step(cols, piece, lower), proto)
    cols, like_scale = column_step(True, row_sums, shape(col_tiles, LANES), shape(*per_block))
    cols = fours(sum_core(cols), "x")
    row_sums, factor = call(
        last_row_kernel, (shape(tall, row_tiles, LANES), shape(col_tiles, LANES)), row_scratch,
        name="rows", ins=(V,) * 6 + (A,),
    )(*cols, stay(upper), stay(lower), stay(like))
    row_sums = exchange(row_sums, proto)

    mine = rank // 2
    row_grad, part_t, factor_mine, factor_other = call(
        functools.partial(gradient_kernel, ratio),
        (
            pltpu.HBM((rows, feat), F32),
            shape(feat, protos),
            shape(mine, protos),
            shape(mine, protos),
        ),
        row_scratch
        + (V((rows, protos), BF16), V((rows, feat), F32), pltpu.SemaphoreType.DMA((blocks,))),
        name="gradient", ins=(V,) * 10, out_specs=(H, V, V, V),
    )(
        stay(like), stay(upper), stay(lower), factor, row_sums, like_scale, feat_t_a, feat_t_b, unit_proto,
        basis_t,
    )
    factor_mine, part_t = lax.optimization_barrier((factor_mine + swap(factor_other, "c", 1), part_t))
    grads = exchange(row_grad.reshape(tall // deep, -1, feat), "y")

    factor_mine, mixed_t = call(
        mixed_kernel, (shape(mine, protos), shape(mine, feat)), name="mixed",
    )(*fours(factor_mine, "x"), part_t, swap(part_t, "c", 1))
    factor_other = swap(factor_mine, "c", 1)
    mixed_t = mixed_t + swap(mixed_t, "z", 1)
    mixed_t = add4(mixed_t, *(swap(mixed_t, "z", m) for m in (2, 6, 4)))
    mixed_other = swap(mixed_t, "c", 1)
    grads = call(gather_kernel, shape(deep * rows // tall, feat), name="gather", ins=(V, A))(
        grads, mixed_t
    )
    mixed_t = jnp.concatenate([mixed_t, mixed_other], axis=0)
    grads = exchange(grads.reshape(deep, rows // tall, feat), "z")
    mixed_t = add4(*fours(mixed_t, "x"))
    proto_grad = call(final_kernel, shape(protos, feat), name="final")(
        *fours(mixed_t, "y"), basis_t, factor_mine, factor_other
    )
    return jnp.sum(grads, axis=0), proto_grad


def solution(mesh):
    wide, tall = mesh.shape["dp"], mesh.shape["proto"]
    fine = Mesh(mesh.devices.reshape(wide // 2, 2, 4, tall // 4), ("x", "c", "y", "z"))
    dp, proto = ("x", "c"), ("y", "z")
    return jax.shard_map(
        on_device,
        mesh=fine,
        in_specs=(P(dp, None), P(proto, None), P(dp), P()),
        out_specs=(P(dp + proto, None), P(proto, None)),
        check_vma=False,
    )
```

```python
import functools
import math

import jax
import jax.numpy as jnp
from jax import lax
from jax.experimental import pallas as pl
from jax.experimental.pallas import tpu as pltpu
from jax.sharding import Mesh, PartitionSpec as P

epsilon = 1e-06
highest = lax.Precision.HIGHEST
F32, BF16 = jnp.float32, jnp.bfloat16
LANES = 128
BLOCK = 256
PIVOTS = 8
MIB = 1 << 20

nt = (((1,), (1,)), ((), ()))
nn = (((1,), (0,)), ((), ()))
tn = (((0,), (0,)), ((), ()))


def dot32(a, b, dims):
    return lax.dot_general(a, b, dims, precision=highest, preferred_element_type=F32)


def dot16(a, b, dims):
    return lax.dot_general(a, b, dims, preferred_element_type=F32)


def split(value):
    high = value.astype(BF16)
    return high, (value - high.astype(F32)).astype(BF16)


def unit_rows(block):
    wide = block.astype(F32)
    return (wide * lax.rsqrt(jnp.sum(wide * wide, axis=-1, keepdims=True) + epsilon)).astype(BF16)


def across(partial):
    count = partial.shape[0] // LANES
    return jnp.concatenate(
        [jnp.sum(partial[i * LANES:(i + 1) * LANES].T, axis=0, keepdims=True) for i in range(count)],
        axis=0,
    )


def down(rows):
    return jnp.concatenate(
        [jnp.broadcast_to(rows[i:i + 1], (LANES, LANES)).T for i in range(rows.shape[0])], axis=0
    )


def tile(j):
    return slice(j * LANES, (j + 1) * LANES)


def fold(value):
    return jnp.sum(value.reshape(-1, 8, LANES), axis=0)


def copies(ref, value):
    for i in range(ref.shape[0]):
        ref[i] = value


def scores_kernel(feat_hbm, proto_hbm, sibling_hbm, seed_hbm, unit_feat, unit_proto, like, col_out, total,
                  sibling, seed_t, feat, proto, ready):
    rows, protos = feat.shape[0], proto.shape[0]
    tiles = protos // LANES
    proto_copy = pltpu.make_async_copy(proto_hbm, proto, ready.at[0])
    feat_copy = pltpu.make_async_copy(feat_hbm, feat, ready.at[1])
    sibling_copy = pltpu.make_async_copy(sibling_hbm, sibling, ready.at[2])
    seed_copy = pltpu.make_async_copy(seed_hbm, seed_t, ready.at[3])
    proto_copy.start()
    feat_copy.start()
    sibling_copy.start()
    seed_copy.start()
    proto_copy.wait()
    unit_proto[...] = unit_rows(proto[...])
    feat_copy.wait()

    cols = [jnp.zeros((8, LANES), F32)] * tiles
    for i in range(rows // BLOCK):
        here = slice(i * BLOCK, (i + 1) * BLOCK)
        unit = unit_rows(feat[here, :])
        unit_feat[here, :] = unit
        value = jnp.exp(dot16(unit, unit_proto[...], nt) * 10.0)
        part = value[:, tile(0)]
        for j in range(1, tiles):
            part = part + value[:, tile(j)]
        total[i] = across(part)
        square = value * value
        like[here, :] = square
        cols = [cols[j] + fold(square[:, tile(j)]) for j in range(tiles)]
    col_out[...] = jnp.concatenate([jnp.sum(c, axis=0, keepdims=True) for c in cols], axis=0)
    sibling_copy.wait()
    seed_copy.wait()


def sibling_kernel(first, unit_feat, unit_proto, sibling, seed_t, after, energy, unit_feat_t, *basis_t):
    rows = unit_feat.shape[0]
    for out in basis_t:
        seed = seed_t[...].astype(F32) * 0.125
        mine = seed.shape[0] // 2
        turned = jnp.concatenate([seed[mine:], seed[:mine]], axis=0)
        out[...] = jnp.where(lax.axis_index("c") == 0, seed, turned)

    for i in range(energy.shape[0] // BLOCK):
        here = slice(i * BLOCK, (i + 1) * BLOCK)
        there = slice(first + i * BLOCK, first + (i + 1) * BLOCK)
        row = lax.broadcasted_iota(jnp.int32, (BLOCK, LANES), 0) + (first + i * BLOCK)
        pick = [
            jnp.where(row == sibling[j:j + 1, :], 1.0, 0.0).astype(BF16) for j in range(rows // LANES)
        ]
        feats = dot16(jnp.concatenate(pick, axis=1), unit_feat[...], nn).astype(BF16)
        energy[here, :] = jnp.exp(dot16(feats, unit_proto[...], nt) * 20.0)
        unit_feat_t[:, here] = unit_feat[there, :].T


def flat(rows):
    return jnp.concatenate([rows[i:i + 1] for i in range(rows.shape[0])], axis=1)


def row_kernel(a, b, c, d, like, rest, later, row_out):
    factor = 1.0 / add4(a[...], b[...], c[...], d[...])
    rows, protos = like.shape
    sums = []
    for i in range(rows // BLOCK):
        part = None
        for j in range(protos // LANES):
            value = like[i * BLOCK:(i + 1) * BLOCK, tile(j)]
            value = value * factor[j:j + 1, :]
            part = value if part is None else part + value
        sums.append(flat(across(part)))
    result = jnp.concatenate(sums, axis=1)
    tall = row_out.shape[0]
    piece = rows // tall
    if rest.shape[0] == 1:
        tails = [rest[...]] * tall
    else:
        totals = rest[...].reshape(rows // LANES, LANES)
        tails = [
            totals[q * piece // LANES:q * piece // LANES + 1, q * piece % LANES:q * piece % LANES + piece]
            for q in range(tall)
        ]
        tails = [jnp.concatenate([t, jnp.zeros((1, LANES - piece), F32)], axis=1) for t in tails]
    for q in range(tall):
        row_out[q] = jnp.concatenate([result, tails[q]], axis=1)


def last_row_kernel(a, b, c, d, upper, lower, like, row_out, factor_out, sums):
    factor = 1.0 / add4(a[...], b[...], c[...], d[...])
    factor_out[...] = factor
    half, protos = upper.shape
    for number, table in enumerate((upper, lower)):
        for i in range(half // BLOCK):
            part = None
            for j in range(protos // LANES):
                value = table[i * BLOCK:(i + 1) * BLOCK, tile(j)] * factor[j:j + 1, :]
                part = value if part is None else part + value
            sums[number * (half // BLOCK) + i] = across(part)
    copies(row_out, sums[...].reshape(row_out.shape[1:]))


def column_kernel(finish, rows_in, like, col_out, extra, scale):
    rows, protos = like.shape
    tall, tiles = rows_in.shape[0], protos // LANES
    sums = rows_in[0]
    for q in range(1, tall):
        sums = sums + rows_in[q]
    inverse_sums = 1.0 / sums[:, :rows]
    for i in range(rows // LANES):
        scale[i // 2, i % 2:i % 2 + 1] = inverse_sums[:, tile(i)]
    if finish:
        piece = rows // tall
        for i in range(rows // LANES):
            each = LANES // piece
            line = [rows_in[each * i + t][:, rows:rows + piece] for t in range(each)]
            extra[i // 2, i % 2:i % 2 + 1] = 10.0 / jnp.concatenate(line, axis=1)
    else:
        extra[...] = sums[:, rows:]

    cols = [jnp.zeros((8, LANES), F32)] * tiles
    for i in range(rows // BLOCK):
        weight = down(scale[i])
        for j in range(tiles):
            value = like[i * BLOCK:(i + 1) * BLOCK, tile(j)]
            cols[j] = cols[j] + fold(value * weight)
    result = jnp.concatenate([jnp.sum(c, axis=0, keepdims=True) for c in cols], axis=0)
    if len(col_out.shape) == 3:
        copies(col_out, result)
    else:
        col_out[...] = result


def predict_kernel(like, total_scale, after, predicted):
    for i in range(like.shape[0] // BLOCK):
        here = slice(i * BLOCK, (i + 1) * BLOCK)
        scale = down(total_scale[i])
        for j in range(like.shape[1] // LANES):
            square = like[here, tile(j)]
            predicted[here, tile(j)] = square * lax.rsqrt(square) * scale


def gradient_kernel(ratio, predicted, upper, lower, factor, rows_in, feat_t_a, feat_t_b, unit_proto, basis_t,
                    row_grad, part_t, factor_mine, factor_other, code_scale, gradient, grads, sent):
    code_scale[...] = (10.0 / jnp.sum(rows_in[...], axis=0)).reshape(code_scale.shape)
    mine = factor_mine.shape[0]
    basis = basis_t[...].astype(BF16)
    rows, protos = predicted.shape
    blocks = rows // BLOCK

    def copy(i):
        here = slice(i * BLOCK, (i + 1) * BLOCK)
        return pltpu.make_async_copy(grads.at[here], row_grad.at[here], sent.at[i])

    for i in range(blocks):
        here = slice(i * BLOCK, (i + 1) * BLOCK)
        table = upper if i < blocks // 2 else lower
        there = slice((i % (blocks // 2)) * BLOCK, (i % (blocks // 2) + 1) * BLOCK)
        second = down(code_scale[i])
        for j in range(protos // LANES):
            value = predicted[here, tile(j)] - table[there, tile(j)] * factor[j:j + 1, :] * second
            gradient[here, tile(j)] = value.astype(BF16)
        grads[here, :] = dot16(gradient[here, :], unit_proto[...], nn)
        copy(i).start()
    for n in range(protos // BLOCK):
        here = slice(n * BLOCK, (n + 1) * BLOCK)
        part = dot16(feat_t_a[...], gradient[:rows // 2, here], nn)
        part = ratio * (part + dot16(feat_t_b[...], gradient[rows // 2:, here], nn))
        part_t[:, here] = part
        high, low = split(part)
        both = dot16(basis, high, nn) + dot16(basis, low, nn)
        factor_mine[:, here] = both[:mine]
        factor_other[:, here] = both[mine:]
    for i in range(blocks):
        copy(i).wait()


def mixed_kernel(a, b, c, d, part_t, part_other, factor_t, mixed_t):
    total = (a[...] + b[...]) + (c[...] + d[...])
    factor_t[...] = total
    rank = total.shape[0]
    part_high, part_low = split(part_t[...] + part_other[...])
    high, low = split(total)
    both = dot16(jnp.concatenate([high, low], axis=0), part_high, nt)
    mixed_t[...] = both[:rank] + both[rank:] + dot16(high, part_low, nt)


def inverse(gram):
    rank = gram.shape[0]
    row = lax.broadcasted_iota(jnp.int32, (rank, 1), 0)
    unit = (row == lax.broadcasted_iota(jnp.int32, (rank, rank), 1)).astype(F32)
    wide = jnp.concatenate([unit, gram, jnp.zeros((rank, LANES - 2 * rank), F32)], axis=1)
    for j in range(0, rank, PIVOTS):
        lines = [wide[j + t:j + t + 1, :] for t in range(PIVOTS)]
        at = [rank + j + t for t in range(PIVOTS)]
        small = [[jnp.broadcast_to(line[:, k:k + 1], (1, LANES)) for k in at] for line in lines]
        columns = [jnp.broadcast_to(wide[:, k:k + 1], (rank, LANES)) for k in at]
        for t in range(PIVOTS):
            scale = 1.0 / small[t][t]
            lines[t] = lines[t] * scale
            small[t] = [v * scale for v in small[t]]
            for u in range(PIVOTS):
                if u != t:
                    by = small[u][t]
                    lines[u] = lines[u] - by * lines[t]
                    small[u] = [v - by * w for v, w in zip(small[u], small[t])]
        reduced = wide
        for t in range(PIVOTS):
            reduced = reduced - columns[t] * lines[t]
        for t in range(PIVOTS):
            reduced = jnp.where(row == j + t, lines[t], reduced)
        wide = reduced
    return wide[:, :rank]


def final_kernel(mixed_a, mixed_b, mixed_c, mixed_d, basis_t, factor_mine, factor_other, proto_grad):
    mixed = (mixed_a[...] + mixed_b[...]) + (mixed_c[...] + mixed_d[...])
    weights = dot32(inverse(dot32(basis_t[...], mixed, nt)), mixed, nn)
    high, low = split(jnp.concatenate([factor_mine[...], factor_other[...]], axis=0))
    weights_high, weights_low = split(weights)
    proto_grad[...] = dot16(
        jnp.concatenate([high, low, high], axis=0),
        jnp.concatenate([weights_high, weights_high, weights_low], axis=0),
        tn,
    )


def gather_kernel(grads, after, out):
    out[...] = jnp.sum(grads[...], axis=0)


def shape(*dims, dtype=F32):
    return jax.ShapeDtypeStruct(dims, dtype)


def kept(*dims, dtype=F32):
    return pltpu.VMEM(dims, dtype)


def stay(value):
    return pltpu.with_memory_space_constraint(value, pltpu.VMEM)


def call(body, outs, scratch=(), limit=24, flops=0, name=None, ins=None, out_specs=None):
    specs = {}
    if ins is not None:
        specs["in_specs"] = [pl.BlockSpec(memory_space=m) for m in ins]
    if out_specs is not None:
        specs["out_specs"] = tuple(pl.BlockSpec(memory_space=m) for m in out_specs)
    return pl.pallas_call(
        body,
        out_shape=outs,
        scratch_shapes=scratch,
        name=name,
        compiler_params=pltpu.CompilerParams(vmem_limit_bytes=limit * MIB),
        cost_estimate=pl.CostEstimate(flops=flops, bytes_accessed=0, transcendentals=0),
        **specs,
    )


def exchange(value, axes):
    return lax.all_to_all(value, axes, 0, 0)


def sum_core(value):
    return value + lax.ppermute(value, "c", [(0, 1), (1, 0)])


def add4(a, b, c, d):
    return (a + b) + (c + d)


def swap(value, axis, mask):
    return lax.ppermute(value, axis, [(i, i ^ mask) for i in range(lax.axis_size(axis))])


def fours(value, axis):
    return (value,) + tuple(swap(value, axis, m) for m in (1, 3, 2))


def on_device(features, prototypes, sibling_view, q_seed):
    proto = ("y", "z")
    rows, feat = features.shape
    protos = prototypes.shape[0]
    rank = q_seed.shape[1]
    half = rows // 2
    row_tiles, col_tiles, blocks = rows // LANES, protos // LANES, rows // BLOCK
    wide, tall = lax.axis_size(("x", "c")), lax.axis_size(proto)
    deep = lax.axis_size("z")
    ratio = (protos * tall) / (rows * wide)
    per_block = (blocks, BLOCK // LANES, LANES)
    row_scratch = (pltpu.VMEM(per_block, F32),)
    V, H, A = pltpu.VMEM, pltpu.HBM, pl.ANY

    unit_feat, unit_proto, like, cols, total, sibling, seed_t = call(
        scores_kernel,
        (
            shape(rows, feat, dtype=BF16),
            shape(protos, feat, dtype=BF16),
            kept(rows, protos),
            shape(col_tiles, LANES),
            shape(*per_block),
            shape(row_tiles, LANES, dtype=jnp.int32),
            shape(rank, feat, dtype=jnp.int32),
        ),
        (V((rows, feat), BF16), V((protos, feat), BF16), pltpu.SemaphoreType.DMA((4,))),
        name="scores", ins=(H, H, H, H),
    )(
        pltpu.with_memory_space_constraint(features, H),
        pltpu.with_memory_space_constraint(prototypes, H),
        pltpu.with_memory_space_constraint(sibling_view.reshape(row_tiles, LANES), H),
        pltpu.with_memory_space_constraint(q_seed.T, H),
    )

    def sibling_half(first, after, *extra):
        return call(
            functools.partial(sibling_kernel, first),
            (kept(half, protos), shape(feat, half, dtype=BF16)) + extra,
            name="sibling", ins=(V, V, V, V, A), flops=4 * half * rows * feat,
        )(unit_feat, unit_proto, sibling, seed_t, after)

    def row_step(cols, rest, later):
        return call(row_kernel, shape(tall, 1, rows + LANES), name="rows", ins=(V,) * 6 + (A,))(
            *cols, stay(like), rest, stay(later)
        )

    def column_step(finish, sums, *outs):
        return call(functools.partial(column_kernel, finish), outs, row_scratch, name="columns")(
            sums, stay(like)
        )

    cols = sum_core(cols)
    upper, feat_t_a, basis_t = sibling_half(0, cols, shape(rank, feat))
    cols = fours(cols, "x")
    row_sums = exchange(row_step(cols, total, upper), proto)
    cols, piece = column_step(False, row_sums, shape(col_tiles, LANES), shape(1, LANES))
    cols = sum_core(cols)
    lower, feat_t_b = sibling_half(half, cols)
    cols = fours(cols, "x")
    row_sums = exchange(row_step(cols, piece, lower), proto)
    cols, like_scale = column_step(True, row_sums, shape(col_tiles, LANES), shape(*per_block))
    cols = sum_core(cols)
    predicted = call(
        predict_kernel, kept(rows, protos), name="predict", ins=(V, V, A), flops=rows * protos * feat
    )(stay(like), like_scale, cols)
    cols = fours(cols, "x")
    row_sums, factor = call(
        last_row_kernel, (shape(tall, row_tiles, LANES), shape(col_tiles, LANES)), row_scratch,
        name="rows", ins=(V,) * 6 + (A,),
    )(*cols, stay(upper), stay(lower), stay(predicted))
    row_sums = exchange(row_sums, proto)

    mine = rank // 2
    row_grad, part_t, factor_mine, factor_other = call(
        functools.partial(gradient_kernel, ratio),
        (
            pltpu.HBM((rows, feat), F32),
            shape(feat, protos),
            shape(mine, protos),
            shape(mine, protos),
        ),
        row_scratch
        + (V((rows, protos), BF16), V((rows, feat), F32), pltpu.SemaphoreType.DMA((blocks,))),
        name="gradient", ins=(V,) * 9, out_specs=(H, V, V, V),
    )(
        stay(predicted), stay(upper), stay(lower), factor, row_sums, feat_t_a, feat_t_b, unit_proto,
        basis_t,
    )
    factor_mine, part_t = lax.optimization_barrier((factor_mine + swap(factor_other, "c", 1), part_t))
    grads = exchange(row_grad.reshape(tall // deep, -1, feat), "y")

    factor_mine, mixed_t = call(
        mixed_kernel, (shape(mine, protos), shape(mine, feat)), name="mixed",
    )(*fours(factor_mine, "x"), part_t, swap(part_t, "c", 1))
    factor_other = swap(factor_mine, "c", 1)
    mixed_t = mixed_t + swap(mixed_t, "z", 1)
    mixed_t = add4(mixed_t, *(swap(mixed_t, "z", m) for m in (2, 6, 4)))
    mixed_other = swap(mixed_t, "c", 1)
    grads = call(gather_kernel, shape(deep * rows // tall, feat), name="gather", ins=(V, A))(
        grads, mixed_t
    )
    mixed_t = jnp.concatenate([mixed_t, mixed_other], axis=0)
    grads = exchange(grads.reshape(deep, rows // tall, feat), "z")
    mixed_t = add4(*fours(mixed_t, "x"))
    proto_grad = call(final_kernel, shape(protos, feat), name="final")(
        *fours(mixed_t, "y"), basis_t, factor_mine, factor_other
    )
    return jnp.sum(grads, axis=0), proto_grad


def solution(mesh):
    wide, tall = mesh.shape["dp"], mesh.shape["proto"]
    fine = Mesh(mesh.devices.reshape(wide // 2, 2, 4, tall // 4), ("x", "c", "y", "z"))
    dp, proto = ("x", "c"), ("y", "z")
    return jax.shard_map(
        on_device,
        mesh=fine,
        in_specs=(P(dp, None), P(proto, None), P(dp), P()),
        out_specs=(P(dp + proto, None), P(proto, None)),
        check_vma=False,
    )
```
